32 devices in a mesh: fsdp: 2 (over x), ctx: 4 (over y, core), tp: 4 (over z).
Axes of the slice: x: 2, y: 2, z: 4, core: 2. Of those that a mesh axis runs over, the one named last changes fastest.
Arguments:
- block_in: bfloat16 [4, 2048, 2048], P('fsdp', 'ctx'), may hold values from -6 to 6
- segments: int32 [4, 2048], P('fsdp'), may hold values from 0 to 16, as said below
- out_grad: bfloat16 [4, 2048, 2048], P('fsdp', 'ctx'), may hold values from -6 to 6
- ln1_gain: bfloat16 [2048], replicated, may hold values from 0.5 to 1.5
- ln1_bias: bfloat16 [2048], replicated, may hold values from -3 to 3
- w_qkv: bfloat16 [2048, 3, 2048], P('fsdp', None, 'tp'), may hold values from -0.125 to 0.125
- b_qv: bfloat16 [2, 2048], P(None, 'tp'), may hold values from -2 to 2
- w_attn_out: bfloat16 [2048, 2048], P('tp', 'fsdp'), may hold values from -0.375 to 0.375
- b_attn_out: bfloat16 [2048], replicated, may hold values from -2 to 2
- ln2_gain: bfloat16 [2048], replicated, may hold values from 0.5 to 1.5
- ln2_bias: bfloat16 [2048], replicated, may hold values from -3 to 3
- w_up: bfloat16 [2048, 8192], P('fsdp', 'tp'), may hold values from -0.125 to 0.125
- b_up: bfloat16 [8192], P('tp'), may hold values from -3 to 3
- w_down: bfloat16 [8192, 2048], P('tp', 'fsdp'), may hold values from -0.0625 to 0.0625
- b_down: bfloat16 [2048], replicated, may hold values from -2 to 2
Outputs:
- block_out: bfloat16 [4, 2048, 2048], P('fsdp', 'ctx')
- in_grad: bfloat16 [4, 2048, 2048], P('fsdp', 'ctx')
- grad_ln1_gain: float32 [2048], replicated
- grad_ln1_bias: float32 [2048], replicated
- grad_w_qkv: float32 [2048, 3, 2048], P('fsdp', None, 'tp')
- grad_b_qv: float32 [2, 2048], P(None, 'tp')
- grad_w_attn_out: float32 [2048, 2048], P('tp', 'fsdp')
- grad_b_attn_out: float32 [2048], replicated
- grad_ln2_gain: float32 [2048], replicated
- grad_ln2_bias: float32 [2048], replicated
- grad_w_up: float32 [2048, 8192], P('fsdp', 'tp')
- grad_b_up: float32 [8192], P('tp')
- grad_w_down: float32 [8192, 2048], P('tp', 'fsdp')
- grad_b_down: float32 [2048], replicated
The draws below stay inside these ranges and needn't reach their ends.
Inputs may be any that keep to these rules, and one draw needn't show every extreme that they name: `segments`: along each sequence the document number starts at 1 and rises by one at each document's end; 0 marks padding, which only follows the documents at the end of a sequence.
All inputs are finite; a program needn't handle non-finite values.
Results may differ from the reference program's by a relative error of at most 0.011.
Values may be sent and summed in bfloat16 or wider, within the bound.
No kernel may reach another device: no remote copies, remote signals or barrier semaphores. Data moves between devices by JAX's collectives and lax.ppermute only.
A program may use at most 320 MiB of HBM per device.

```python
import jax
import jax.numpy as jnp
from jax import lax

D = 2048
FF = 8192
H = 16
HD = 128
SEQ = 2048
SEQS = 4


def draw_segments(key, part):
    key = jax.random.fold_in(key, 11)
    sub_keys = jax.random.split(key, 3)
    pieces = 15
    short_cap = max(SEQ // 64, 2)
    upper = short_cap.bit_length() - 1
    exponent = jax.random.randint(sub_keys[0], (SEQS, pieces), 0, upper)
    lower_size = jnp.power(2, exponent).astype(jnp.int32)
    sizes = lower_size + jax.random.randint(sub_keys[1], (SEQS, pieces), 0, lower_size)
    ends = jnp.cumsum(sizes, axis=1)
    positions = jnp.arange(SEQ)
    doc_ids = 1 + jnp.sum((positions[None, :, None] >= ends[:, None, :]).astype(jnp.int32), axis=2)
    pad_from = SEQ - jax.random.randint(sub_keys[2], (SEQS, 1), 0, SEQ // 8 + 1)
    doc_ids = jnp.where(positions[None, :] >= pad_from, 0, doc_ids)
    return doc_ids.astype(jnp.int32)


def block_scale(own_key, extent, cuts, least, largest):
    gain, own = 1.0, jax.random.fold_in(own_key, 6)
    for dim, shards_of in cuts:
        heights = jnp.exp(jax.random.uniform(jax.random.fold_in(own, dim), (shards_of,), jnp.float32, least / len(cuts), largest / len(cuts)))
        gain = gain * jnp.repeat(heights, extent[dim] // shards_of).reshape([-1 if axis == dim else 1 for axis in range(len(extent))])
    return gain


def normal_values(own_key, dims, scale, reach, cuts=(), held_as=jnp.bfloat16):
    loudness = block_scale(own_key, dims, cuts, -0.22, 0.18) if cuts else 1.0
    result = jax.random.normal(own_key, dims, jnp.float32) * scale * loudness
    return jnp.minimum(jnp.maximum(result, -reach), reach).astype(held_as)


def setup_inputs(seed: int = 0) -> dict:
    key_of = jax.random.split(jax.random.key(seed), 16)
    block_in = normal_values(key_of[0], (SEQS, SEQ, D), 1.0, 6.0, ((0, 2), (1, 4)))
    segments = draw_segments(jax.random.fold_in(key_of[15], 71), 0)
    out_grad = normal_values(key_of[2], (SEQS, SEQ, D), 1.0, 6.0, ((0, 2), (1, 4)))
    ln1_gain = jnp.clip(1.0 + 0.1 * jax.random.normal(key_of[3], (D,), jnp.float32), 0.5, 1.5).astype(jnp.bfloat16)
    ln1_bias = normal_values(key_of[4], (D,), 0.5, 3.0)
    w_qkv = normal_values(key_of[5], (D, 3, D), D ** -0.5, 0.125, ((0, 2), (2, 4)))
    b_qv = normal_values(key_of[6], (2, D), 0.3, 2.0, ((1, 4),))
    w_attn_out = normal_values(key_of[7], (D, D), (D // 8) ** -0.5, 0.375, ((0, 4), (1, 2)))
    b_attn_out = normal_values(key_of[8], (D,), 0.3, 2.0)
    ln2_gain = jnp.clip(1.0 + 0.1 * jax.random.normal(key_of[9], (D,), jnp.float32), 0.5, 1.5).astype(jnp.bfloat16)
    ln2_bias = normal_values(key_of[10], (D,), 0.5, 3.0)
    w_up = normal_values(key_of[11], (D, FF), D ** -0.5, 0.125, ((0, 2), (1, 4)))
    b_up = normal_values(key_of[12], (FF,), 0.5, 3.0, ((0, 4),))
    w_down = normal_values(key_of[13], (FF, D), FF ** -0.5, 0.0625, ((0, 4), (1, 2)))
    b_down = normal_values(key_of[14], (D,), 0.3, 2.0)
    return dict(block_in=block_in, segments=segments, out_grad=out_grad, ln1_gain=ln1_gain, ln1_bias=ln1_bias, w_qkv=w_qkv, b_qv=b_qv, w_attn_out=w_attn_out, b_attn_out=b_attn_out, ln2_gain=ln2_gain, ln2_bias=ln2_bias, w_up=w_up, b_up=b_up, w_down=w_down, b_down=b_down)


NORM_EPS = 1e-05
MASKED = -1e+30
HIGHEST = lax.Precision.HIGHEST

@jax.custom_vjp
def low(v):
    return lax.optimization_barrier(v.astype(jnp.bfloat16)).astype(jnp.float32)

@jax.custom_vjp
def low_back(v):
    return v

def low_keep(v):
    return (low(v), None)

def low_pass(kept, grad):
    return (grad,)

def back_keep(v):
    return (v, None)

def back_low(kept, grad):
    return (low(grad),)
low.defvjp(low_keep, low_pass)
low_back.defvjp(back_keep, back_low)

def norm_parts(values):
    centred = values - lax.optimization_barrier(jnp.mean(values, axis=-1, keepdims=True))
    return centred * lax.rsqrt(lax.optimization_barrier(jnp.mean(centred * centred, axis=-1, keepdims=True)) + NORM_EPS)

def attend_one(batch_item):
    queries, keys, values, seg_ids = batch_item
    positions = jnp.arange(seg_ids.shape[0])
    allowed = (seg_ids[:, None] == seg_ids[None, :]) & (positions[None, :] <= positions[:, None])
    scores = low_back(jnp.einsum('qhe,khe->hqk', queries, keys, precision=HIGHEST) * HD ** (-0.5))
    scores = jnp.where(allowed[None], scores, MASKED)
    row_max = lax.optimization_barrier(jnp.max(scores, axis=-1, keepdims=True))
    exp_scores = jnp.exp(scores - row_max)
    probs = exp_scores / lax.optimization_barrier(jnp.sum(exp_scores, axis=-1, keepdims=True))
    return jnp.einsum('hqk,khe->qhe', low(probs), values, precision=HIGHEST)

def forward(block, seg_ids, gain_one, shift_one, w_qkv, b_qv, w_out, b_out, gain_two, shift_two, w_up, b_up, w_down, b_down):
    input_one = low(norm_parts(block) * gain_one + shift_one)
    projected = jnp.einsum('gtd,dcf->gtcf', input_one, w_qkv, precision=HIGHEST)
    head_shape = block.shape[:2] + (H, HD)
    queries = low(low_back(projected[:, :, 0] + b_qv[0])).reshape(head_shape)
    keys = low(low_back(projected[:, :, 1])).reshape(head_shape)
    values = low(low_back(projected[:, :, 2] + b_qv[1])).reshape(head_shape)
    attended = lax.map(jax.checkpoint(attend_one), (queries, keys, values, seg_ids))
    attended = low(low_back(attended.reshape(block.shape)))
    middle = block + low_back(jnp.einsum('gtf,fd->gtd', attended, w_out, precision=HIGHEST) + b_out)
    input_two = low(norm_parts(middle) * gain_two + shift_two)
    hidden = low_back(jnp.einsum('gtd,df->gtf', input_two, w_up, precision=HIGHEST) + b_up)
    active = low(jax.nn.gelu(hidden, approximate=True))
    return middle + low_back(jnp.einsum('gtf,fd->gtd', active, w_down, precision=HIGHEST) + b_down)

def reference(block_in, segments, out_grad, ln1_gain, ln1_bias, w_qkv, b_qv, w_attn_out, b_attn_out, ln2_gain, ln2_bias, w_up, b_up, w_down, b_down):
    params = tuple((p.astype(jnp.float32) for p in (ln1_gain, ln1_bias, w_qkv, b_qv, w_attn_out, b_attn_out, ln2_gain, ln2_bias, w_up, b_up, w_down, b_down)))
    valid_rows = (segments != 0).astype(jnp.float32)
    cotan = out_grad.astype(jnp.float32) * valid_rows[:, :, None]
    pair_count = SEQS // 2
    inputs = (block_in.astype(jnp.float32).reshape(pair_count, 2, SEQ, D), segments.reshape(pair_count, 2, SEQ), cotan.reshape(pair_count, 2, SEQ, D))

    def step(totals, batch_item):
        block, seg_ids, cot_rows = batch_item

        def run(block_vals, *weights):
            return forward(block_vals, seg_ids, *weights)
        layer_out, pullback = jax.vjp(run, block, *params)
        gradients = pullback(cot_rows)
        summed = tuple((running + added for running, added in zip(totals, gradients[1:])))
        return (summed, (layer_out.astype(jnp.bfloat16), gradients[0].astype(jnp.bfloat16)))
    totals, (outputs, input_grads) = lax.scan(step, tuple((jnp.zeros_like(p) for p in params)), inputs)
    return (outputs.reshape(SEQS, SEQ, D), input_grads.reshape(SEQS, SEQ, D), totals[0], totals[1], totals[2], totals[3], totals[4], totals[5], totals[6], totals[7], totals[8], totals[9], totals[10], totals[11])
```

```python
import jax
import jax.numpy as jnp
from jax import lax
from jax.sharding import PartitionSpec as P

HD = 128
NORM_EPS = 1e-05
MASKED = -1e30
F32 = jnp.float32
BF16 = jnp.bfloat16

X_SWAP = [(0, 1), (1, 0)]


def xor_pairs(count, bit):
    return [(j, j ^ bit) for j in range(count)]


def core_swap(values):
    return lax.ppermute(values, "ctx", xor_pairs(lax.axis_size("ctx"), 1))


def y_swap(values):
    return lax.ppermute(values, "ctx", xor_pairs(lax.axis_size("ctx"), 2))


def x_swap(values):
    return lax.ppermute(values, "fsdp", X_SWAP)


def norm_parts(values):
    centred = values - jnp.mean(values, axis=-1, keepdims=True)
    norm_scale = lax.rsqrt(jnp.mean(centred * centred, axis=-1, keepdims=True) + NORM_EPS)
    return (centred * norm_scale, norm_scale)


def norm_back(grad_norm, gain, normed, norm_scale):
    lifted = grad_norm * gain
    return norm_scale * (
        lifted
        - jnp.mean(lifted, axis=-1, keepdims=True)
        - normed * jnp.mean(lifted * normed, axis=-1, keepdims=True)
    )


def gelu_tanh(values):
    return jax.nn.gelu(values, approximate=True)


def piece(values, start, count, axis):
    return lax.dynamic_slice_in_dim(values, start, count, axis)


def dot(a, b):
    return jnp.dot(a, b, preferred_element_type=F32)


def dot_t(a, b):
    return lax.dot_general(a, b, (((1,), (1,)), ((), ())), preferred_element_type=F32)


def t_dot(a, b):
    return lax.dot_general(a, b, (((0,), (0,)), ((), ())), preferred_element_type=F32)


def to_relative(values):
    i, c = lax.axis_index("fsdp"), lax.axis_index("ctx") & 1
    size = values.shape[-1] // 4
    axis = values.ndim - 1
    return jnp.concatenate(
        [piece(values, (((k & 1) ^ i) * 2 + ((k >> 1) ^ c)) * size, size, axis) for k in range(4)],
        axis=axis,
    )


def to_natural(values):
    i, c = lax.axis_index("fsdp"), lax.axis_index("ctx") & 1
    size = values.shape[-1] // 4
    axis = values.ndim - 1
    return jnp.concatenate(
        [piece(values, (((b >> 1) ^ i) + 2 * ((b & 1) ^ c)) * size, size, axis) for b in range(4)],
        axis=axis,
    )


def roll_rows(values):
    n = lax.axis_size("tp")
    z = lax.axis_index("tp")
    size = values.shape[0] // n
    return jnp.concatenate(
        [piece(values, lax.rem(z + k, n) * size, size, 0) for k in range(n)], axis=0
    )


def gather_weight(values, axis):
    c = lax.axis_index("ctx") & 1
    size = values.shape[axis] // 2
    mine_c = piece(values, c * size, size, axis)
    mine_n = piece(values, (1 - c) * size, size, axis)
    other_c = x_swap(mine_c)
    other_n = core_swap(other_c)
    return jnp.concatenate([mine_c, other_c, mine_n, other_n], axis=axis)


def reduce_weight(values, axis):
    c = lax.axis_index("ctx") & 1
    size = values.shape[axis] // 4

    def cut(array, k, count):
        return lax.slice_in_dim(array, k * size, (k + count) * size, axis=axis)

    got = core_swap(cut(values, 2, 2))
    pair = cut(values, 0, 2).astype(F32) + got.astype(F32)
    got = x_swap(cut(pair, 1, 1).astype(BF16))
    four = lax.optimization_barrier((cut(pair, 0, 1) + got.astype(F32)).astype(BF16))
    got = y_swap(four)
    total = lax.optimization_barrier((four.astype(F32) + got.astype(F32)).astype(BF16))
    other = core_swap(total)
    first = jnp.where(c == 0, total, other)
    second = jnp.where(c == 0, other, total)
    return jnp.concatenate([first, second], axis=axis).astype(F32)


def line_reduce(partial):
    n = lax.axis_size("tp")
    size = partial.shape[0] // n

    def block(k):
        return partial[k * size : (k + 1) * size]

    ahead = behind = None
    for step in range(1, n):
        up, down = block(n - step), block(step)
        if ahead is not None:
            up = (up.astype(F32) + ahead.astype(F32)).astype(BF16)
            down = (down.astype(F32) + behind.astype(F32)).astype(BF16)
        ahead = lax.ppermute(up, "tp", [(j, j + 1) for j in range(step)])
        behind = lax.ppermute(down, "tp", [(n - 1 - j, n - 2 - j) for j in range(step)])
    total = block(0).astype(F32)
    if ahead is not None:
        total = total + ahead.astype(F32) + behind.astype(F32)
    return total


def line_gather(own):
    n = lax.axis_size("tp")
    z = lax.axis_index("tp")
    ahead, behind = [own], [own]
    for k in range(1, n):
        ahead.append(lax.ppermute(ahead[-1], "tp", [(j, j + 1) for j in range(k - 1, n - 1)]))
        behind.append(lax.ppermute(behind[-1], "tp", [(j, j - 1) for j in range(1, n - k + 1)]))
    return [own] + [jnp.where(z + k < n, behind[k], ahead[n - k]) for k in range(1, n)]


def natural_rows(blocks):
    n = len(blocks)
    z = lax.axis_index("tp")
    size = blocks[0].shape[0]
    doubled = jnp.concatenate(blocks, axis=0)
    return jnp.concatenate(
        [piece(doubled, lax.rem(j - z + n, n) * size, size, 0) for j in range(n)], axis=0
    )


def scores_of(queries, keys, allowed):
    raw = jnp.einsum("qhe,khe->hqk", queries, keys, preferred_element_type=F32) * HD ** (-0.5)
    return jnp.where(allowed[None], raw, MASKED)


def attend(queries, keys, values, allowed):
    scores = scores_of(queries, keys, allowed)
    row_max = jnp.max(scores, axis=-1, keepdims=True)
    exp_scores = jnp.exp(scores - row_max)
    row_total = jnp.sum(exp_scores, axis=-1, keepdims=True)
    weights = (exp_scores / row_total).astype(BF16)
    attended = jnp.einsum("hqk,khe->qhe", weights, values, preferred_element_type=F32)
    return attended.astype(BF16), row_max + jnp.log(row_total)


def attend_back(queries, keys, values, allowed, log_total, grad_att):
    scores = scores_of(queries, keys, allowed)
    probs = jnp.exp(scores - log_total)
    probs_low = probs.astype(BF16)
    grad_values = jnp.einsum("hqk,qhe->khe", probs_low, grad_att, preferred_element_type=F32)
    grad_probs = jnp.einsum("qhe,khe->hqk", grad_att, values, preferred_element_type=F32)
    grad_scores = (
        probs * (grad_probs - jnp.sum(probs * grad_probs, axis=-1, keepdims=True))
    ).astype(BF16)
    factor = HD ** (-0.5)
    grad_queries = jnp.einsum("hqk,khe->qhe", grad_scores, keys, preferred_element_type=F32)
    grad_keys = jnp.einsum("hqk,qhe->khe", grad_scores, queries, preferred_element_type=F32)
    return (
        (grad_queries * factor).astype(BF16),
        (grad_keys * factor).astype(BF16),
        grad_values.astype(BF16),
    )


def sum_pairs(values, tp_too):
    values = values + core_swap(values)
    values = values + y_swap(values)
    values = values + x_swap(values)
    if tp_too:
        n = lax.axis_size("tp")
        bit = 1
        while bit < n:
            values = values + lax.ppermute(values, "tp", xor_pairs(n, bit))
            bit *= 2
    return values


def local(
    block_in,
    segments,
    out_grad,
    ln1_gain,
    ln1_bias,
    w_qkv,
    b_qv,
    w_attn_out,
    b_attn_out,
    ln2_gain,
    ln2_bias,
    w_up,
    b_up,
    w_down,
    b_down,
):
    seqs, span, width = block_in.shape
    n = lax.axis_size("tp")
    cx = lax.axis_index("ctx")
    blocks = lax.axis_size("ctx")
    part = span // n
    local_width = w_qkv.shape[2]
    heads = local_width // HD
    each = range(seqs)

    wk = gather_weight(w_qkv[:, 1], 0)
    wv = gather_weight(w_qkv[:, 2], 0)
    wq = gather_weight(w_qkv[:, 0], 0)
    wo = gather_weight(w_attn_out, 1)
    wu = gather_weight(w_up, 0)
    wd = gather_weight(w_down, 1)

    gain_one = to_relative(ln1_gain.astype(F32))
    shift_one = to_relative(ln1_bias.astype(F32))
    gain_two = to_relative(ln2_gain.astype(F32))
    shift_two = to_relative(ln2_bias.astype(F32))
    bias_out = to_relative(b_attn_out.astype(F32))
    bias_down = to_relative(b_down.astype(F32))
    bias_q, bias_v = b_qv[0].astype(F32), b_qv[1].astype(F32)
    bias_up = b_up.astype(F32)

    spot = lax.rem(lax.axis_index("tp") * part + jnp.arange(span), span)

    x_rows, n1, queries, kv_all, allowed, cot = [], [], [], [], [], []
    for s in each:
        rows = to_relative(roll_rows(block_in[s]))
        x_rows.append(rows)
        normed, unused = norm_parts(rows.astype(F32))
        n1.append((normed * gain_one + shift_one).astype(BF16))
    for s in each:
        keys_here = dot(n1[s], wk).astype(BF16)
        values_here = (dot(n1[s], wv) + bias_v).astype(BF16)
        kv = jnp.concatenate([keys_here, values_here], axis=1)
        kv1 = core_swap(kv)
        kv2 = y_swap(kv)
        kv3 = core_swap(kv2)
        kv_all.append(jnp.concatenate([kv, kv1, kv2, kv3], axis=0))
    for s in each:
        queries.append((dot(n1[s], wq) + bias_q).astype(BF16))
        query_seg = roll_rows(piece(segments[s], cx * span, span, 0))
        key_seg = jnp.concatenate(
            [roll_rows(piece(segments[s], (cx ^ b) * span, span, 0)) for b in range(blocks)]
        )
        key_pos = jnp.concatenate([(cx ^ b) * span + spot for b in range(blocks)])
        allowed.append(
            (query_seg[:, None] == key_seg[None, :])
            & (key_pos[None, :] <= (cx * span + spot)[:, None])
        )
        valid = (query_seg != 0).astype(BF16)[:, None]
        cot.append(to_relative(roll_rows(out_grad[s])) * valid)

    def heads_of(values):
        return values.reshape(values.shape[0], heads, HD)

    def halves(s):
        return heads_of(kv_all[s][:, :local_width]), heads_of(kv_all[s][:, local_width:])

    attended, log_total, middle = [], [], []
    n2 = []
    for s in each:
        keys, values = halves(s)
        out, total = attend(heads_of(queries[s]), keys, values, allowed[s])
        attended.append(out.reshape(span, local_width))
        log_total.append(total)
        summed = line_reduce(dot(attended[s], wo).astype(BF16))
        mid = x_rows[s][:part].astype(F32) + summed + bias_out
        middle.append(mid)
        normed, unused = norm_parts(mid)
        own = (normed * gain_two + shift_two).astype(BF16)
        n2.append(jnp.concatenate(line_gather(own), axis=0))

    active, grad_hidden, kept_two, gm = [], [], [], []
    out_rows = []
    for s in each:
        hidden = dot(n2[s], wu) + bias_up
        act, pull = jax.vjp(gelu_tanh, hidden)
        active.append(act.astype(BF16))
        grad_hidden.append(pull(dot_t(cot[s], wd))[0].astype(BF16))
        summed = line_reduce(dot_t(grad_hidden[s], wu).astype(BF16))
        normed, norm_scale = norm_parts(middle[s])
        grad_mid = cot[s][:part].astype(F32) + norm_back(summed, gain_two, normed, norm_scale)
        own = grad_mid.astype(BF16)
        kept_two.append((grad_mid, summed, normed, own))
        gm.append(jnp.concatenate(line_gather(own), axis=0))
    for s in each:
        summed = line_reduce(dot(active[s], wd).astype(BF16))
        own = to_natural((middle[s] + summed + bias_down).astype(BF16))
        out_rows.append(natural_rows(line_gather(own)))

    grads, kept_one, in_rows = [], [], []
    for s in each:
        grad_att = dot_t(gm[s], wo).astype(BF16)
        keys, values = halves(s)
        gq, gk, gv = attend_back(
            heads_of(queries[s]), keys, values, allowed[s], log_total[s], heads_of(grad_att)
        )
        gq = gq.reshape(span, local_width)
        gkv = jnp.concatenate(
            [gk.reshape(blocks, span, local_width), gv.reshape(blocks, span, local_width)], axis=2
        )
        got = core_swap(jnp.stack([gkv[1], gkv[3]]))
        far = (gkv[2].astype(F32) + got[1].astype(F32)).astype(BF16)
        near = gkv[0].astype(F32) + got[0].astype(F32)
        total = (near + y_swap(far).astype(F32)).astype(BF16)
        gk, gv = total[:, :local_width], total[:, local_width:]
        grads.append((gq, gk, gv))
        summed = line_reduce((dot_t(gq, wq) + dot_t(gk, wk) + dot_t(gv, wv)).astype(BF16))
        normed, norm_scale = norm_parts(x_rows[s][:part].astype(F32))
        grad_in = kept_two[s][0] + norm_back(summed, gain_one, normed, norm_scale)
        kept_one.append((summed, normed))
        own = to_natural(grad_in.astype(BF16))
        in_rows.append(natural_rows(line_gather(own)))

    def stack(items):
        return jnp.concatenate(list(items), axis=0)

    n1_all, n2_all = stack(n1), stack(n2)
    g_down = reduce_weight(t_dot(stack(active), stack(cot)).astype(BF16), 1)
    g_up = reduce_weight(t_dot(n2_all, stack(grad_hidden)).astype(BF16), 0)
    g_out = reduce_weight(t_dot(stack(attended), stack(gm)).astype(BF16), 1)
    g_qkv = jnp.stack(
        [reduce_weight(t_dot(n1_all, stack(g[k] for g in grads)).astype(BF16), 0) for k in range(3)],
        axis=1,
    )

    def over_rows(items):
        return sum(jnp.sum(item.astype(F32), axis=0) for item in items)

    wide = [
        over_rows([kept_one[s][0] * kept_one[s][1] for s in each]),
        over_rows([kept_one[s][0] for s in each]),
        over_rows([kept_two[s][3] for s in each]),
        over_rows([kept_two[s][1] * kept_two[s][2] for s in each]),
        over_rows([kept_two[s][1] for s in each]),
        over_rows([cot[s][:part] for s in each]),
    ]
    wide_sum = sum_pairs(to_natural(jnp.stack(wide)), True)
    narrow = jnp.concatenate(
        [
            over_rows([g[0] for g in grads]),
            over_rows([g[2] for g in grads]),
            over_rows(grad_hidden),
        ]
    )
    narrow_sum = sum_pairs(narrow, False)
    g_bqv = narrow_sum[: 2 * local_width].reshape(2, local_width)
    g_bup = narrow_sum[2 * local_width :]
    return (
        jnp.stack(out_rows),
        jnp.stack(in_rows),
        wide_sum[0],
        wide_sum[1],
        g_qkv,
        g_bqv,
        g_out,
        wide_sum[2],
        wide_sum[3],
        wide_sum[4],
        g_up,
        g_bup,
        g_down,
        wide_sum[5],
    )


def solution(mesh):
    in_specs = (
        P("fsdp", "ctx", None),
        P("fsdp", None),
        P("fsdp", "ctx", None),
        P(),
        P(),
        P("fsdp", None, "tp"),
        P(None, "tp"),
        P("tp", "fsdp"),
        P(),
        P(),
        P(),
        P("fsdp", "tp"),
        P("tp"),
        P("tp", "fsdp"),
        P(),
    )
    out_specs = (
        P("fsdp", "ctx", None),
        P("fsdp", "ctx", None),
        P(),
        P(),
        P("fsdp", None, "tp"),
        P(None, "tp"),
        P("tp", "fsdp"),
        P(),
        P(),
        P(),
        P("fsdp", "tp"),
        P("tp"),
        P("tp", "fsdp"),
        P(),
    )
    return jax.shard_map(local, mesh=mesh, in_specs=in_specs, out_specs=out_specs, check_vma=False)
```

```python
import jax
import jax.numpy as jnp
from jax import lax
from jax.experimental import pallas as pl
from jax.experimental.pallas import tpu as pltpu
from jax.sharding import PartitionSpec as P

HD = 128
NORM_EPS = 1e-05
MASKED = -1e30
LOG2E = 1.4426950408889634
F32 = jnp.float32
BF16 = jnp.bfloat16

X_SWAP = [(0, 1), (1, 0)]


def xor_pairs(count, bit):
    return [(j, j ^ bit) for j in range(count)]


def core_swap(values):
    return lax.ppermute(values, "ctx", xor_pairs(lax.axis_size("ctx"), 1))


def y_swap(values):
    return lax.ppermute(values, "ctx", xor_pairs(lax.axis_size("ctx"), 2))


def x_swap(values):
    return lax.ppermute(values, "fsdp", X_SWAP)


def norm_parts(values):
    centred = values - jnp.mean(values, axis=-1, keepdims=True)
    norm_scale = lax.rsqrt(jnp.mean(centred * centred, axis=-1, keepdims=True) + NORM_EPS)
    return (centred * norm_scale, norm_scale)


def norm_back(grad_norm, gain, normed, norm_scale):
    lifted = grad_norm * gain
    return norm_scale * (
        lifted
        - jnp.mean(lifted, axis=-1, keepdims=True)
        - normed * jnp.mean(lifted * normed, axis=-1, keepdims=True)
    )


def gelu_tanh(values):
    return jax.nn.gelu(values, approximate=True)


def piece(values, start, count, axis):
    return lax.dynamic_slice_in_dim(values, start, count, axis)


def dot(a, b):
    return jnp.dot(a, b, preferred_element_type=F32)


def dot_t(a, b):
    return lax.dot_general(a, b, (((1,), (1,)), ((), ())), preferred_element_type=F32)


def t_dot(a, b):
    return lax.dot_general(a, b, (((0,), (0,)), ((), ())), preferred_element_type=F32)


def to_relative(values):
    i, c = lax.axis_index("fsdp"), lax.axis_index("ctx") & 1
    size = values.shape[-1] // 4
    axis = values.ndim - 1
    return jnp.concatenate(
        [piece(values, (((k & 1) ^ i) * 2 + ((k >> 1) ^ c)) * size, size, axis) for k in range(4)],
        axis=axis,
    )


def to_natural(values):
    i, c = lax.axis_index("fsdp"), lax.axis_index("ctx") & 1
    size = values.shape[-1] // 4
    axis = values.ndim - 1
    return jnp.concatenate(
        [piece(values, (((b >> 1) ^ i) + 2 * ((b & 1) ^ c)) * size, size, axis) for b in range(4)],
        axis=axis,
    )


def mix_rows(values):
    n = lax.axis_size("tp")
    z = lax.axis_index("tp")
    size = values.shape[0] // n
    return jnp.concatenate([piece(values, (z ^ k) * size, size, 0) for k in range(n)], axis=0)


def gather_weight(values, axis):
    c = lax.axis_index("ctx") & 1
    size = values.shape[axis] // 2
    mine_c = piece(values, c * size, size, axis)
    mine_n = piece(values, (1 - c) * size, size, axis)
    other_c = x_swap(mine_c)
    other_n = core_swap(other_c)
    return jnp.concatenate([mine_c, other_c, mine_n, other_n], axis=axis)


def reduce_weight(values, axis):
    c = lax.axis_index("ctx") & 1
    size = values.shape[axis] // 4

    def cut(array, k, count):
        return lax.slice_in_dim(array, k * size, (k + count) * size, axis=axis)

    got = core_swap(cut(values, 2, 2))
    pair = cut(values, 0, 2).astype(F32) + got.astype(F32)
    got = x_swap(cut(pair, 1, 1).astype(BF16))
    four = lax.optimization_barrier((cut(pair, 0, 1) + got.astype(F32)).astype(BF16))
    got = y_swap(four)
    total = lax.optimization_barrier((four.astype(F32) + got.astype(F32)).astype(BF16))
    other = core_swap(total)
    first = jnp.where(c == 0, total, other)
    second = jnp.where(c == 0, other, total)
    return jnp.concatenate([first, second], axis=axis).astype(F32)


def tp_swap(values, bit):
    return lax.ppermute(values, "tp", xor_pairs(lax.axis_size("tp"), bit))


def line_reduce(partial):
    n = lax.axis_size("tp")
    size = partial.shape[0] // n
    blocks = [partial[k * size : (k + 1) * size] for k in range(n)]
    if n == 4:
        got = tp_swap(blocks[3], 1)
        passed = (blocks[2].astype(F32) + got.astype(F32)).astype(BF16)
        far = tp_swap(passed, 2)
        near = tp_swap(blocks[1], 1)
        return blocks[0].astype(F32) + near.astype(F32) + far.astype(F32)
    bit = 1
    order = list(range(n))
    held = dict(zip(order, blocks))
    while bit < n:
        away = [k for k in held if k & bit]
        got = tp_swap(jnp.concatenate([held[k] for k in away], axis=0), bit)
        for j, k in enumerate(away):
            summed = held[k ^ bit].astype(F32) + got[j * size : (j + 1) * size].astype(F32)
            held[k ^ bit] = summed.astype(BF16)
            del held[k]
        bit *= 2
    return held[0].astype(F32)


def line_gather(own):
    n = lax.axis_size("tp")
    if n == 4:
        far = tp_swap(own, 2)
        near = tp_swap(own, 1)
        return [own, near, far, tp_swap(far, 1)]
    blocks = [own]
    bit = 1
    while bit < n:
        size = own.shape[0]
        got = tp_swap(jnp.concatenate(blocks, axis=0), bit)
        blocks = blocks + [got[k * size : (k + 1) * size] for k in range(bit)]
        bit *= 2
    return blocks


def natural_rows(blocks):
    n = len(blocks)
    z = lax.axis_index("tp")
    size = blocks[0].shape[0]
    mixed = jnp.concatenate(blocks, axis=0)
    return jnp.concatenate([piece(mixed, (j ^ z) * size, size, 0) for j in range(n)], axis=0)


def fwd_kernel(live, q, kv0, kv1, kv2, kv3, kseg, qseg, kpos, qpos, out, lse, m_s, l_s, acc_s):
    queries = q[...]
    rate = HD ** (-0.5) * LOG2E

    def scores(kv, b):
        t = dot_t(kv[0], queries) * rate
        allowed = kseg[b] == qseg[...]
        if b == 0:
            allowed = allowed & (kpos[...] <= qpos[...])
        return jnp.where(allowed, t, MASKED)

    t = scores(kv0, 0)
    top = jnp.max(t, axis=0, keepdims=True)
    p = jnp.exp2(t - top)
    m_s[...] = top
    l_s[...] = jnp.sum(p, axis=0, keepdims=True)
    acc_s[...] = t_dot(kv0[1], p.astype(BF16))
    for b, kv in ((1, kv1), (2, kv2), (3, kv3)):

        @pl.when(live[b] > 0)
        def _(b=b, kv=kv):
            t = scores(kv, b)
            old = m_s[...]
            top = jnp.maximum(old, jnp.max(t, axis=0, keepdims=True))
            p = jnp.exp2(t - top)
            fade = jnp.exp2(old - top)
            m_s[...] = top
            l_s[...] = l_s[...] * fade + jnp.sum(p, axis=0, keepdims=True)
            acc_s[...] = acc_s[...] * fade + t_dot(kv[1], p.astype(BF16))

    total = l_s[...]
    out[...] = (acc_s[...] / total).T.astype(BF16)
    lse[0] = m_s[...] + jnp.log2(total)


def bwd_kernel(
    live, q, kv0, kv1, kv2, kv3, kseg, qseg, kpos, qpos, att, grad, lse, gq, near, far, gq_s
):
    queries = q[...]
    rate = HD ** (-0.5) * LOG2E
    factor = HD ** (-0.5)
    grad_out = grad[...]
    product = grad_out.astype(F32) * att[...].astype(F32)
    delta = jnp.sum(product.T, axis=0, keepdims=True)
    total = lse[0]

    def grads(kv, b):
        t = dot_t(kv[0], queries) * rate
        allowed = kseg[b] == qseg[...]
        if b == 0:
            allowed = allowed & (kpos[...] <= qpos[...])
        p = jnp.exp2(jnp.where(allowed, t, MASKED) - total)
        gv = dot(p.astype(BF16), grad_out)
        gp = dot_t(kv[1], grad_out)
        gs = (p * (gp - delta)).astype(BF16)
        gk = dot(gs, queries) * factor
        return gk.astype(BF16), gv.astype(BF16), t_dot(kv[0], gs)

    gk, gv, turned = grads(kv0, 0)
    near[0, 0] = gk
    near[0, 1] = gv
    gq_s[...] = turned
    for b, kv, place, slot in ((1, kv1, far, 0), (2, kv2, near, 1), (3, kv3, far, 1)):

        @pl.when(live[b] > 0)
        def _(b=b, kv=kv, place=place, slot=slot):
            gk, gv, turned = grads(kv, b)
            place[slot, 0] = gk
            place[slot, 1] = gv
            gq_s[...] += turned

        @pl.when(live[b] == 0)
        def _(place=place, slot=slot):
            place[slot] = jnp.zeros(place.shape[1:], BF16)

    gq[...] = (gq_s[...] * factor).T.astype(BF16)


def attend_specs(span):
    def whole(*shape):
        return pl.BlockSpec(shape, lambda h, *_: (0,) * len(shape))

    head = pl.BlockSpec((span, HD), lambda h, *_: (0, h))
    pair = pl.BlockSpec((2, span, HD), lambda h, *_: (0, 0, h))
    stat = pl.BlockSpec((1, 1, span), lambda h, *_: (h, 0, 0))
    both = pl.BlockSpec((2, 2, span, HD), lambda h, *_: (0, 0, 0, h))
    ins = [head] + [pair] * 4 + [whole(4, span, 1), whole(1, span), whole(span, 1), whole(1, span)]
    return head, stat, both, ins


def attend(live, queries, kvs, marks):
    span, local_width = queries.shape
    heads = local_width // HD
    head, stat, both, ins = attend_specs(span)
    return pl.pallas_call(
        fwd_kernel,
        grid_spec=pltpu.PrefetchScalarGridSpec(
            num_scalar_prefetch=1,
            grid=(heads,),
            in_specs=ins,
            out_specs=[head, stat],
            scratch_shapes=[
                pltpu.VMEM((1, span), F32),
                pltpu.VMEM((1, span), F32),
                pltpu.VMEM((HD, span), F32),
            ],
        ),
        out_shape=[
            jax.ShapeDtypeStruct((span, local_width), BF16),
            jax.ShapeDtypeStruct((heads, 1, span), F32),
        ],
        compiler_params=pltpu.CompilerParams(vmem_limit_bytes=48 * 2**20),
        cost_estimate=pl.CostEstimate(
            flops=16 * heads * span * span * HD,
            bytes_accessed=10 * span * local_width * 2,
            transcendentals=4 * heads * span * span,
        ),
        name="attend",
    )(live, queries, *kvs, *marks)


def attend_back(live, queries, kvs, marks, attended, grad_att, log_total):
    span, local_width = queries.shape
    heads = local_width // HD
    head, stat, both, ins = attend_specs(span)
    return pl.pallas_call(
        bwd_kernel,
        grid_spec=pltpu.PrefetchScalarGridSpec(
            num_scalar_prefetch=1,
            grid=(heads,),
            in_specs=ins + [head, head, stat],
            out_specs=[head, both, both],
            scratch_shapes=[pltpu.VMEM((HD, span), F32)],
        ),
        out_shape=[
            jax.ShapeDtypeStruct((span, local_width), BF16),
            jax.ShapeDtypeStruct((2, 2, span, local_width), BF16),
            jax.ShapeDtypeStruct((2, 2, span, local_width), BF16),
        ],
        compiler_params=pltpu.CompilerParams(vmem_limit_bytes=48 * 2**20),
        cost_estimate=pl.CostEstimate(
            flops=40 * heads * span * span * HD,
            bytes_accessed=20 * span * local_width * 2,
            transcendentals=4 * heads * span * span,
        ),
        name="attend_back",
    )(live, queries, *kvs, *marks, attended, grad_att, log_total)


def sum_pairs(values, tp_too):
    values = values + core_swap(values)
    values = values + y_swap(values)
    values = values + x_swap(values)
    if tp_too:
        n = lax.axis_size("tp")
        bit = 1
        while bit < n:
            values = values + lax.ppermute(values, "tp", xor_pairs(n, bit))
            bit *= 2
    return values


def local(
    block_in,
    segments,
    out_grad,
    ln1_gain,
    ln1_bias,
    w_qkv,
    b_qv,
    w_attn_out,
    b_attn_out,
    ln2_gain,
    ln2_bias,
    w_up,
    b_up,
    w_down,
    b_down,
):
    seqs, span, width = block_in.shape
    n = lax.axis_size("tp")
    cx = lax.axis_index("ctx")
    blocks = lax.axis_size("ctx")
    part = span // n
    local_width = w_qkv.shape[2]
    each = range(seqs)

    wk = gather_weight(w_qkv[:, 1], 0)
    wv = gather_weight(w_qkv[:, 2], 0)
    wq = gather_weight(w_qkv[:, 0], 0)
    wo = gather_weight(w_attn_out, 1)
    wu = gather_weight(w_up, 0)
    wd = gather_weight(w_down, 1)

    gain_one = to_relative(ln1_gain.astype(F32))
    shift_one = to_relative(ln1_bias.astype(F32))
    gain_two = to_relative(ln2_gain.astype(F32))
    shift_two = to_relative(ln2_bias.astype(F32))
    bias_out = to_relative(b_attn_out.astype(F32))
    bias_down = to_relative(b_down.astype(F32))
    bias_q, bias_v = b_qv[0].astype(F32), b_qv[1].astype(F32)
    bias_up = b_up.astype(F32)

    spot = mix_rows(jnp.arange(span, dtype=jnp.int32))
    live = jnp.stack([((cx ^ b) <= cx).astype(jnp.int32) for b in range(blocks)])

    x_rows, n1, queries, kv_all, marks, cot = [], [], [], [], [], []
    for s in each:
        rows = to_relative(mix_rows(block_in[s]))
        x_rows.append(rows)
        normed, unused = norm_parts(rows.astype(F32))
        n1.append((normed * gain_one + shift_one).astype(BF16))
    for s in each:
        keys_here = dot(n1[s], wk).astype(BF16)
        values_here = (dot(n1[s], wv) + bias_v).astype(BF16)
        kv = jnp.stack([keys_here, values_here])
        kv1 = core_swap(kv)
        kv2 = y_swap(kv)
        kv3 = core_swap(kv2)
        kv_all.append((kv, kv1, kv2, kv3))
    for s in each:
        queries.append((dot(n1[s], wq) + bias_q).astype(BF16))
        key_seg = jnp.stack(
            [mix_rows(piece(segments[s], (cx ^ b) * span, span, 0)) for b in range(blocks)]
        )
        marks.append((key_seg[:, :, None], key_seg[0][None, :], spot[:, None], spot[None, :]))
        valid = (key_seg[0] != 0).astype(BF16)[:, None]
        cot.append(to_relative(mix_rows(out_grad[s])) * valid)

    attended, log_total, middle = [], [], []
    n2 = []
    for s in each:
        out, total = attend(live, queries[s], kv_all[s], marks[s])
        attended.append(out)
        log_total.append(total)
        summed = line_reduce(dot(attended[s], wo).astype(BF16))
        mid = x_rows[s][:part].astype(F32) + summed + bias_out
        middle.append(mid)
        normed, unused = norm_parts(mid)
        own = (normed * gain_two + shift_two).astype(BF16)
        n2.append(jnp.concatenate(line_gather(own), axis=0))

    active, grad_hidden, kept_two, gm = [], [], [], []
    out_rows = []
    for s in each:
        hidden = dot(n2[s], wu) + bias_up
        act, pull = jax.vjp(gelu_tanh, hidden)
        active.append(act.astype(BF16))
        grad_hidden.append(pull(dot_t(cot[s], wd))[0].astype(BF16))
        summed = line_reduce(dot_t(grad_hidden[s], wu).astype(BF16))
        normed, norm_scale = norm_parts(middle[s])
        grad_mid = cot[s][:part].astype(F32) + norm_back(summed, gain_two, normed, norm_scale)
        own = grad_mid.astype(BF16)
        kept_two.append((grad_mid, summed, normed, own))
        gm.append(jnp.concatenate(line_gather(own), axis=0))
    for s in each:
        summed = line_reduce(dot(active[s], wd).astype(BF16))
        own = to_natural((middle[s] + summed + bias_down).astype(BF16))
        out_rows.append(natural_rows(line_gather(own)))

    grads, kept_one, in_rows = [], [], []
    for s in each:
        grad_att = dot_t(gm[s], wo).astype(BF16)
        gq, near, away = attend_back(
            live, queries[s], kv_all[s], marks[s], attended[s], grad_att, log_total[s]
        )
        got = core_swap(away)
        far = (near[1].astype(F32) + got[1].astype(F32)).astype(BF16)
        total = near[0].astype(F32) + got[0].astype(F32)
        total = (total + y_swap(far).astype(F32)).astype(BF16)
        gk, gv = total[0], total[1]
        grads.append((gq, gk, gv))
        summed = line_reduce((dot_t(gq, wq) + dot_t(gk, wk) + dot_t(gv, wv)).astype(BF16))
        normed, norm_scale = norm_parts(x_rows[s][:part].astype(F32))
        grad_in = kept_two[s][0] + norm_back(summed, gain_one, normed, norm_scale)
        kept_one.append((summed, normed))
        own = to_natural(grad_in.astype(BF16))
        in_rows.append(natural_rows(line_gather(own)))

    def stack(items):
        return jnp.concatenate(list(items), axis=0)

    n1_all, n2_all = stack(n1), stack(n2)
    g_down = reduce_weight(t_dot(stack(active), stack(cot)).astype(BF16), 1)
    g_up = reduce_weight(t_dot(n2_all, stack(grad_hidden)).astype(BF16), 0)
    g_out = reduce_weight(t_dot(stack(attended), stack(gm)).astype(BF16), 1)
    g_qkv = jnp.stack(
        [reduce_weight(t_dot(n1_all, stack(g[k] for g in grads)).astype(BF16), 0) for k in range(3)],
        axis=1,
    )

    def over_rows(items):
        return sum(jnp.sum(item.astype(F32), axis=0) for item in items)

    wide = [
        over_rows([kept_one[s][0] * kept_one[s][1] for s in each]),
        over_rows([kept_one[s][0] for s in each]),
        over_rows([kept_two[s][3] for s in each]),
        over_rows([kept_two[s][1] * kept_two[s][2] for s in each]),
        over_rows([kept_two[s][1] for s in each]),
        over_rows([cot[s][:part] for s in each]),
    ]
    wide_sum = sum_pairs(to_natural(jnp.stack(wide)), True)
    narrow = jnp.concatenate(
        [
            over_rows([g[0] for g in grads]),
            over_rows([g[2] for g in grads]),
            over_rows(grad_hidden),
        ]
    )
    narrow_sum = sum_pairs(narrow, False)
    g_bqv = narrow_sum[: 2 * local_width].reshape(2, local_width)
    g_bup = narrow_sum[2 * local_width :]
    return (
        jnp.stack(out_rows),
        jnp.stack(in_rows),
        wide_sum[0],
        wide_sum[1],
        g_qkv,
        g_bqv,
        g_out,
        wide_sum[2],
        wide_sum[3],
        wide_sum[4],
        g_up,
        g_bup,
        g_down,
        wide_sum[5],
    )


def solution(mesh):
    in_specs = (
        P("fsdp", "ctx", None),
        P("fsdp", None),
        P("fsdp", "ctx", None),
        P(),
        P(),
        P("fsdp", None, "tp"),
        P(None, "tp"),
        P("tp", "fsdp"),
        P(),
        P(),
        P(),
        P("fsdp", "tp"),
        P("tp"),
        P("tp", "fsdp"),
        P(),
    )
    out_specs = (
        P("fsdp", "ctx", None),
        P("fsdp", "ctx", None),
        P(),
        P(),
        P("fsdp", None, "tp"),
        P(None, "tp"),
        P("tp", "fsdp"),
        P(),
        P(),
        P(),
        P("fsdp", "tp"),
        P("tp"),
        P("tp", "fsdp"),
        P(),
    )
    return jax.shard_map(local, mesh=mesh, in_specs=in_specs, out_specs=out_specs, check_vma=False)
```

```python
import jax
import jax.numpy as jnp
from jax import lax
from jax.experimental import pallas as pl
from jax.experimental.pallas import tpu as pltpu
from jax.sharding import PartitionSpec as P

HD = 128
NORM_EPS = 1e-05
MASKED = -1e30
LOG2E = 1.4426950408889634
F32 = jnp.float32
BF16 = jnp.bfloat16

ROOM = 44 * 2**20
X_SWAP = [(0, 1), (1, 0)]
ANY = pl.BlockSpec(memory_space=pl.ANY)


def xor_pairs(count, bit):
    return [(j, j ^ bit) for j in range(count)]


def core_swap(values):
    return lax.ppermute(values, "ctx", xor_pairs(lax.axis_size("ctx"), 1))


def y_swap(values):
    return lax.ppermute(values, "ctx", xor_pairs(lax.axis_size("ctx"), 2))


def x_swap(values):
    return lax.ppermute(values, "fsdp", X_SWAP)


def tp_swap(values, bit):
    return lax.ppermute(values, "tp", xor_pairs(lax.axis_size("tp"), bit))


def norm_parts(values):
    centred = values - jnp.mean(values, axis=-1, keepdims=True)
    norm_scale = lax.rsqrt(jnp.mean(centred * centred, axis=-1, keepdims=True) + NORM_EPS)
    return (centred * norm_scale, norm_scale)


def norm_back(grad_norm, gain, normed, norm_scale):
    lifted = grad_norm * gain
    return norm_scale * (
        lifted
        - jnp.mean(lifted, axis=-1, keepdims=True)
        - normed * jnp.mean(lifted * normed, axis=-1, keepdims=True)
    )


def dot(a, b):
    return jnp.dot(a, b, preferred_element_type=F32)


def dot_t(a, b):
    return lax.dot_general(a, b, (((1,), (1,)), ((), ())), preferred_element_type=F32)


def t_dot(a, b):
    return lax.dot_general(a, b, (((0,), (0,)), ((), ())), preferred_element_type=F32)


def piece(values, start, count, axis):
    return lax.dynamic_slice_in_dim(values, start, count, axis)


def to_relative(values):
    i, c = lax.axis_index("fsdp"), lax.axis_index("ctx") & 1
    size = values.shape[-1] // 4
    axis = values.ndim - 1
    return jnp.concatenate(
        [piece(values, (((k & 1) ^ i) * 2 + ((k >> 1) ^ c)) * size, size, axis) for k in range(4)],
        axis=axis,
    )


def to_natural(values):
    i, c = lax.axis_index("fsdp"), lax.axis_index("ctx") & 1
    size = values.shape[-1] // 4
    axis = values.ndim - 1
    return jnp.concatenate(
        [piece(values, (((b >> 1) ^ i) + 2 * ((b & 1) ^ c)) * size, size, axis) for b in range(4)],
        axis=axis,
    )


def mix_rows(values):
    n = lax.axis_size("tp")
    z = lax.axis_index("tp")
    size = values.shape[0] // n
    return jnp.concatenate([piece(values, (z ^ k) * size, size, 0) for k in range(n)], axis=0)


class Order:
    def __init__(self, place):
        self.place = place
        self.last = None

    def call(self, body, name, grid, ins, outs, scratch=(), flops=0, after=(), alias=None):
        spare = list(after)
        if self.last is not None and self.last is not alias:
            spare.append(self.last)
        if alias is not None:
            spare.append(alias)
        first = 1 + len(ins)

        def kernel(*refs):
            body(*refs[:first], *refs[first + len(spare) :])

        moved = sum(a.size * a.dtype.itemsize for a, unused in ins)
        moved += sum(2 * jnp.dtype(d).itemsize * len(s) for s, d, unused in outs)
        result = pl.pallas_call(
            kernel,
            grid_spec=pltpu.PrefetchScalarGridSpec(
                num_scalar_prefetch=1,
                grid=grid,
                in_specs=[spec for unused, spec in ins] + [ANY] * len(spare),
                out_specs=[spec for unused, also, spec in outs],
                scratch_shapes=list(scratch),
            ),
            out_shape=[jax.ShapeDtypeStruct(s, d) for s, d, unused in outs],
            input_output_aliases={} if alias is None else {len(ins) + len(spare): 0},
            compiler_params=pltpu.CompilerParams(vmem_limit_bytes=ROOM),
            cost_estimate=pl.CostEstimate(
                flops=int(flops), bytes_accessed=int(moved), transcendentals=0
            ),
            name=name,
        )(self.place, *[a for a, unused in ins], *spare)
        self.last = result[-1]
        return result

    def tie(self, *values):
        count = len(values)

        def kernel(place, *refs):
            del place, refs

        tied = pl.pallas_call(
            kernel,
            grid_spec=pltpu.PrefetchScalarGridSpec(
                num_scalar_prefetch=1,
                grid=(1,),
                in_specs=[ANY] * (count + 1),
                out_specs=[ANY] * count,
            ),
            out_shape=[jax.ShapeDtypeStruct(a.shape, a.dtype) for a in values],
            input_output_aliases={1 + k: k for k in range(count)},
            name="tie",
        )(self.place, *values, self.last)
        self.last = tied[0]
        return tied if count > 1 else tied[0]


def whole(shape):
    return pl.BlockSpec(shape, lambda *_: (0,) * len(shape))


def natural_of(place, k):
    return ((k & 1) ^ place[1]) * 2 + ((k >> 1) ^ place[0])


def own_half(place, which):
    return place[0] if which == 0 else 1 - place[0]


def take_half(order, weight, base, count, axis, after=()):
    unused, rows, cols = weight.shape
    if axis == 0:
        rows = rows // 2
    else:
        cols = cols // 2
    tile = min(rows, 512)

    def body(place, src, dst):
        dst[...] = src[...]

    def spot(g, i, place):
        if axis == 0:
            return (base + g, place[0] * (rows // tile) + i, 0)
        return (base + g, i, place[0])

    block = (1, tile, cols)
    return order.call(
        body,
        "take_half",
        (count, rows // tile),
        [(weight, pl.BlockSpec(block, spot))],
        [((count, rows, cols), BF16, pl.BlockSpec(block, lambda g, i, place: (g, i, 0)))],
        after=after,
    )[0]


def norm_in(order, block_in, gain, shift, n):
    seqs, span, width = block_in.shape
    part = span // n
    size = width // 4

    def body(place, src, gain_ref, shift_ref, normed_ref, own_ref, line):
        for k in range(n):
            rows = pl.ds(pl.multiple_of((place[2] ^ k) * part, part), part)
            for s in range(seqs):
                values = src[s, rows, :].astype(F32)
                normed, unused = norm_parts(values)
                line[...] = (normed * gain_ref[...] + shift_ref[...]).astype(BF16)
                to = (k * seqs + s) * part
                for p in range(4):
                    cols = pl.ds(pl.multiple_of(natural_of(place, p) * size, size), size)
                    normed_ref[to : to + part, p * size : (p + 1) * size] = line[:, cols]
                    if k == 0:
                        own_ref[to : to + part, p * size : (p + 1) * size] = src[s, rows, cols]

    return order.call(
        body,
        "norm_in",
        (1,),
        [
            (block_in, whole(block_in.shape)),
            (gain, whole((1, width))),
            (shift, whole((1, width))),
        ],
        [
            ((seqs * span, width), BF16, whole((seqs * span, width))),
            ((seqs * part, width), BF16, whole((seqs * part, width))),
        ],
        [pltpu.VMEM((part, width), BF16)],
    )


def cot_in(order, out_grad, valid, n):
    seqs, span, width = out_grad.shape
    part = span // n
    size = width // 4

    def body(place, src, valid_ref, cot_ref):
        for k in range(n):
            rows = pl.ds(pl.multiple_of((place[2] ^ k) * part, part), part)
            for s in range(seqs):
                to = (k * seqs + s) * part
                for p in range(4):
                    cols = pl.ds(pl.multiple_of(natural_of(place, p) * size, size), size)
                    values = src[s, rows, cols].astype(F32) * valid_ref[s, rows, :]
                    cot_ref[to : to + part, p * size : (p + 1) * size] = values.astype(BF16)

    shape = (seqs * span, width)
    return order.call(
        body,
        "cot_in",
        (1,),
        [(out_grad, whole(out_grad.shape)), (valid, whole(valid.shape))],
        [(shape, BF16, whole(shape))],
    )[0]


def by_sequence(values, n, seqs):
    rows, width = values.shape
    return values.reshape(n, seqs, rows // n // seqs, width)


def project(order, n1, weights, base, far_c, far_n, bias, name):
    count, size, local = far_c.shape
    one = isinstance(n1, tuple)
    if one:
        values, s = n1
        n, unused, part, width = values.shape
        rows = n * part
        spec = pl.BlockSpec((n, 1, part, width), lambda g, place: (0, s, 0, 0))
    else:
        values = n1
        rows, width = values.shape
        spec = whole((rows, width))

    def body(place, x, a, b, c, d, bias_ref, out):
        total = bias_ref[0].astype(F32)
        for p, ref in enumerate((a, b, c, d)):
            cols = slice(p * size, (p + 1) * size)
            some = x[:, 0, :, cols].reshape(rows, size) if one else x[:, cols]
            total = total + dot(some, ref[0])
        out[0] = total.astype(BF16)

    block = (1, size, local)
    near = [
        pl.BlockSpec(block, lambda g, place, h=h: (base + g, own_half(place, h), 0)) for h in (0, 1)
    ]
    away = pl.BlockSpec(block, lambda g, place: (g, 0, 0))
    return order.call(
        body,
        name,
        (count,),
        [
            (values, spec),
            (weights, near[0]),
            (far_c, away),
            (weights, near[1]),
            (far_n, away),
            (bias, pl.BlockSpec((1, 1, local), lambda g, place: (g, 0, 0))),
        ],
        [((count, rows, local), BF16, pl.BlockSpec((1, rows, local), lambda g, place: (g, 0, 0)))],
        flops=2 * rows * width * local * count,
    )[0]


def row_ins(parts, part, width):
    return [
        (array, pl.BlockSpec((part, width), lambda *_, k=k: (k, 0))) for array, k in parts
    ]


def row_outs(n, block, width):
    counts = (2, 1, 1) if n == 4 else (n // 2, n // 2)
    return [((c * block, width), BF16, whole((c * block, width))) for c in counts]


def put_rows(outs, block, n, cols, rows):
    for k in range(n):
        which, spot = (k % 2, k // 2)
        if n == 4 and which:
            which, spot = 1 + spot, 0
        outs[which][spot * block : (spot + 1) * block, cols] = rows[k * block : (k + 1) * block]


def col_pieces(weight, far_c, far_n, tile):
    unused, units, size = far_c.shape
    steps = size // tile
    block = (1, units, tile)
    near = [
        pl.BlockSpec(block, lambda g, place, h=h: (0, 0, own_half(place, h) * steps + g))
        for h in (0, 1)
    ]
    away = pl.BlockSpec(block, lambda g, place: (0, 0, g))
    return [(weight, near[0]), (far_c, away), (weight, near[1]), (far_n, away)], steps


def row_pieces(weight, far_c, far_n, tile):
    unused, size, units = far_c.shape
    steps = size // tile
    block = (1, tile, units)
    near = [
        pl.BlockSpec(block, lambda g, place, h=h: (0, own_half(place, h) * steps + g, 0))
        for h in (0, 1)
    ]
    away = pl.BlockSpec(block, lambda g, place: (0, g, 0))
    return [(weight, near[0]), (far_c, away), (weight, near[1]), (far_n, away)], steps


def to_features(order, values, pieces, steps, tile, turned, n, width, name, seqs=None):
    rows, units = values.shape
    block = rows // n
    size = width // 4
    times = dot_t if turned else dot

    def body(place, x, a, b, c, d, *outs):
        g = pl.program_id(0)
        for p, ref in enumerate((a, b, c, d)):
            got = times(x[...], ref[0]).astype(BF16)
            cols = pl.ds(pl.multiple_of(p * size + g * tile, tile), tile)
            if not seqs:
                put_rows(outs, block, n, cols, got)
                continue
            part = block // seqs
            for k in range(n):
                spot = pl.ds(pl.multiple_of((place[2] ^ k) * part, part), part)
                for s in range(seqs):
                    start = k * block + s * part
                    outs[0][s, spot, cols] = got[start : start + part]

    outs = row_outs(n, block, width)
    if seqs:
        shape = (seqs, rows // seqs, width)
        outs = [(shape, BF16, whole(shape))]
    return order.call(
        body,
        name,
        (steps,),
        [(values, whole((rows, units)))] + pieces,
        outs,
        flops=2 * rows * units * width,
    )


def add_rows(order, a, b, block):
    width = a[0].shape[1]

    def body(place, x, y, out):
        out[...] = (x[...].astype(F32) + y[...].astype(F32)).astype(BF16)

    return order.call(
        body,
        "add_rows",
        (1,),
        row_ins([a, b], block, width),
        [((block, width), BF16, whole((block, width)))],
    )[0]


def sum_all(refs):
    total = refs[0][...].astype(F32)
    for ref in refs[1:]:
        total = total + ref[...].astype(F32)
    return total


def norm_mid(order, parts, own, bias, gain, shift):
    part, width = own.shape
    count = len(parts)

    def body(place, *refs):
        own_ref, bias_ref, gain_ref, shift_ref, mid_ref, normed_ref = refs[count:]
        mid = own_ref[...].astype(F32) + sum_all(refs[:count]) + bias_ref[...]
        mid_ref[...] = mid
        normed, unused = norm_parts(mid)
        normed_ref[...] = (normed * gain_ref[...] + shift_ref[...]).astype(BF16)

    block, line = whole((part, width)), whole((1, width))
    return order.call(
        body,
        "norm_mid",
        (1,),
        row_ins(parts, part, width) + [(own, block), (bias, line), (gain, line), (shift, line)],
        [((part, width), F32, block), ((part, width), BF16, block)],
    )


def back_mid(order, parts, mid, cot, gain):
    part, width = mid.shape
    count = len(parts)

    def body(place, *refs):
        mid_ref, cot_ref, gain_ref, stats, grad_ref, low_ref = refs[count:]
        g2 = sum_all(refs[:count])
        normed, norm_scale = norm_parts(mid_ref[...])
        cotan = cot_ref[...].astype(F32)
        grad = cotan + norm_back(g2, gain_ref[...], normed, norm_scale)
        low = grad.astype(BF16)
        grad_ref[...] = grad
        low_ref[...] = low
        rows = (low.astype(F32), g2 * normed, g2, cotan)
        for k, values in enumerate(rows):
            stats[k : k + 1, :] = jnp.sum(values, axis=0, keepdims=True)
        stats[4:8, :] = jnp.zeros((4, width), F32)

    block, line = whole((part, width)), whole((1, width))
    return order.call(
        body,
        "back_mid",
        (1,),
        row_ins(parts, part, width) + [(mid, block), (cot, block), (gain, line)],
        [
            ((8, width), F32, whole((8, width))),
            ((part, width), F32, block),
            ((part, width), BF16, block),
        ],
    )


def back_in(order, parts, own, grad_mid, gain):
    part, width = own.shape
    count = len(parts)
    size = width // 4

    def body(place, *refs):
        own_ref, mid_ref, gain_ref, stats, low_ref, line = refs[count:]
        g1 = sum_all(refs[:count])
        normed, norm_scale = norm_parts(own_ref[...].astype(F32))
        grad = mid_ref[...] + norm_back(g1, gain_ref[...], normed, norm_scale)
        line[...] = grad.astype(BF16)
        for p in range(4):
            cols = pl.ds(pl.multiple_of(natural_of(place, p) * size, size), size)
            low_ref[:, cols] = line[:, p * size : (p + 1) * size]
        for k, values in enumerate((g1 * normed, g1)):
            stats[k : k + 1, :] = jnp.sum(values, axis=0, keepdims=True)
        stats[2:8, :] = jnp.zeros((6, width), F32)

    block, line = whole((part, width)), whole((1, width))
    return order.call(
        body,
        "back_in",
        (1,),
        row_ins(parts, part, width) + [(own, block), (grad_mid, block), (gain, line)],
        [((8, width), F32, whole((8, width))), ((part, width), BF16, block)],
        [pltpu.VMEM((part, width), BF16)],
    )


def gather_rows(refs, store):
    part = refs[0].shape[0]
    for k, ref in enumerate(refs):
        store[k * part : (k + 1) * part, :] = ref[...]


def active_grad(order, cot, weight, far_c, far_n):
    span, width = cot.shape
    units = weight.shape[1]
    size = width // 4
    tile = min(units, 512)

    def body(place, x, a, b, c, d, out):
        total = dot_t(x[:, :size], a[0])
        for p, ref in enumerate((b, c, d)):
            total = total + dot_t(x[:, (p + 1) * size : (p + 2) * size], ref[0])
        out[...] = total

    block = (1, tile, size)
    near = [pl.BlockSpec(block, lambda g, place, h=h: (0, g, own_half(place, h))) for h in (0, 1)]
    away = pl.BlockSpec(block, lambda g, place: (0, g, 0))
    return order.call(
        body,
        "active_grad",
        (units // tile,),
        [
            (cot, whole((span, width))),
            (weight, near[0]),
            (far_c, away),
            (weight, near[1]),
            (far_n, away),
        ],
        [((span, units), F32, pl.BlockSpec((span, tile), lambda g, place: (0, g)))],
        flops=2 * span * units * width,
    )[0]


def feed(order, n2_parts, weight, far_c, far_n, bias, grad_active):
    n = len(n2_parts)
    width = n2_parts[0][0].shape[1]
    span = cot_rows = grad_active.shape[0]
    part = cot_rows // n
    units = weight.shape[2]
    size = width // 4
    tile = min(units, 512)

    def body(place, *refs):
        a, b, c, d, bias_ref, ga_ref, sums, act_ref, gh_ref, x = refs[n:]

        @pl.when(pl.program_id(0) == 0)
        def _():
            gather_rows(refs[:n], x)

        rate = 0.7978845608028654
        step = min(tile, 256)
        for start in range(0, tile, step):
            cols = slice(start, start + step)
            hidden = bias_ref[:, cols] + dot(x[:, :size], a[0, :, cols])
            for p, ref in enumerate((b, c, d)):
                hidden = hidden + dot(x[:, (p + 1) * size : (p + 2) * size], ref[0, :, cols])
            square = hidden * hidden
            bend = jnp.tanh(hidden * (rate + rate * 0.044715 * square))
            half = 0.5 + 0.5 * bend
            act_ref[:, cols] = (hidden * half).astype(BF16)
            turn = half - half * bend
            slope = half + hidden * turn * (rate + rate * 0.134145 * square)
            gh = (ga_ref[:, cols] * slope).astype(BF16)
            gh_ref[:, cols] = gh
            sums[:, cols] = jnp.sum(gh.astype(F32), axis=0, keepdims=True)

    block = (1, size, tile)
    near = [pl.BlockSpec(block, lambda g, place, h=h: (0, own_half(place, h), g)) for h in (0, 1)]
    away = pl.BlockSpec(block, lambda g, place: (0, 0, g))
    cols = pl.BlockSpec((span, tile), lambda g, place: (0, g))
    line = pl.BlockSpec((1, tile), lambda g, place: (0, g))
    return order.call(
        body,
        "feed",
        (units // tile,),
        row_ins(n2_parts, part, width)
        + [
            (weight, near[0]),
            (far_c, away),
            (weight, near[1]),
            (far_n, away),
            (bias, line),
            (grad_active, cols),
        ],
        [((1, units), F32, line), ((span, units), BF16, cols), ((span, units), BF16, cols)],
        [pltpu.VMEM((span, width), BF16)],
        flops=2 * span * units * width,
    )


def heads_grad(order, gm_parts, span, weight, far_c, far_n):
    n = len(gm_parts)
    width = gm_parts[0][0].shape[1]
    part = span // n
    local = weight.shape[1]
    size = width // 4

    def body(place, *refs):
        a, b, c, d, out, x = refs[n:]
        gather_rows(refs[:n], x)
        total = dot_t(x[:, :size], a[0])
        for p, ref in enumerate((b, c, d)):
            total = total + dot_t(x[:, (p + 1) * size : (p + 2) * size], ref[0])
        out[...] = total.astype(BF16)

    pieces, unused = col_pieces(weight, far_c, far_n, size)
    return order.call(
        body,
        "heads_grad",
        (1,),
        row_ins(gm_parts, part, width) + pieces,
        [((span, local), BF16, whole((span, local)))],
        [pltpu.VMEM((span, width), BF16)],
        flops=2 * span * local * width,
    )[0]


def head_rows(ref, h):
    n, unused, part, size = ref.shape
    return ref[:, 0, :, h * HD : (h + 1) * HD].reshape(n * part, HD)


def put_head(ref, h, turned):
    n, unused, part, size = ref.shape
    ref[:, 0, :, h * HD : (h + 1) * HD] = turned.T.astype(BF16).reshape(n, part, HD)


def head_of(kv, j, h):
    return kv[j, :, h * HD : (h + 1) * HD]


def fwd_kernel(live, q, kv0, kv1, kv2, kv3, kseg, qseg, kpos, qpos, out, lse, m_s, l_s, acc_s):
    heads = range(q.shape[3] // HD)
    rate = HD ** (-0.5) * LOG2E

    def scores(kv, b, h):
        t = dot_t(head_of(kv, 0, h), head_rows(q, h)) * rate
        allowed = kseg[b] == qseg[...]
        if b == 0:
            allowed = allowed & (kpos[...] <= qpos[...])
        return jnp.where(allowed, t, MASKED)

    for h in heads:
        t = scores(kv0, 0, h)
        top = jnp.max(t, axis=0, keepdims=True)
        p = jnp.exp2(t - top)
        m_s[h] = top
        l_s[h] = jnp.sum(p, axis=0, keepdims=True)
        acc_s[h] = t_dot(head_of(kv0, 1, h), p.astype(BF16))
    for b, kv in ((1, kv1), (2, kv2), (3, kv3)):

        @pl.when(live[4 + b] > 0)
        def _(b=b, kv=kv):
            for h in heads:
                t = scores(kv, b, h)
                old = m_s[h]
                top = jnp.maximum(old, jnp.max(t, axis=0, keepdims=True))
                p = jnp.exp2(t - top)
                fade = jnp.exp2(old - top)
                m_s[h] = top
                l_s[h] = l_s[h] * fade + jnp.sum(p, axis=0, keepdims=True)
                acc_s[h] = acc_s[h] * fade + t_dot(head_of(kv, 1, h), p.astype(BF16))

    for h in heads:
        total = l_s[h]
        put_head(out, h, acc_s[h] / total)
        lse[h] = m_s[h] + jnp.log2(total)


def bwd_kernel(
    live,
    q,
    kv0,
    kv1,
    kv2,
    kv3,
    kseg,
    qseg,
    kpos,
    qpos,
    att,
    grad,
    lse,
    gq,
    near,
    far,
    gq_s,
    delta_s,
):
    heads = range(q.shape[3] // HD)
    rate = HD ** (-0.5) * LOG2E
    factor = HD ** (-0.5)

    def grads(kv, b, h):
        queries, grad_out, keys = head_rows(q, h), head_rows(grad, h), head_of(kv, 0, h)
        t = dot_t(keys, queries) * rate
        allowed = kseg[b] == qseg[...]
        if b == 0:
            allowed = allowed & (kpos[...] <= qpos[...])
        p = jnp.exp2(jnp.where(allowed, t, MASKED) - lse[h])
        gv = dot(p.astype(BF16), grad_out)
        gp = dot_t(head_of(kv, 1, h), grad_out)
        gs = (p * (gp - delta_s[h])).astype(BF16)
        gk = dot(gs, queries) * factor
        return gk.astype(BF16), gv.astype(BF16), t_dot(keys, gs)

    def put(place, slot, h, gk, gv):
        cols = slice(h * HD, (h + 1) * HD)
        place[slot, 0, :, cols] = gk
        place[slot, 1, :, cols] = gv

    for h in heads:
        product = head_rows(grad, h).astype(F32) * head_rows(att, h).astype(F32)
        delta_s[h] = jnp.sum(product.T, axis=0, keepdims=True)
    for h in heads:
        gk, gv, turned = grads(kv0, 0, h)
        put(near, 0, h, gk, gv)
        gq_s[h] = turned
    for b, kv, place, slot in ((1, kv1, far, 0), (2, kv2, near, 1), (3, kv3, far, 1)):

        @pl.when(live[4 + b] > 0)
        def _(b=b, kv=kv, place=place, slot=slot):
            for h in heads:
                gk, gv, turned = grads(kv, b, h)
                put(place, slot, h, gk, gv)
                gq_s[h] += turned

        @pl.when(live[4 + b] == 0)
        def _(place=place, slot=slot):
            place[slot] = jnp.zeros(place.shape[1:], BF16)

    for h in heads:
        put_head(gq, h, gq_s[h] * factor)


def attend_ins(queries, s, kvs, marks):
    n, unused, part, local = queries.shape
    span = n * part
    heads = local // HD
    some = min(heads, 2)
    cols = some * HD
    head = pl.BlockSpec((n, 1, part, cols), lambda h, *_: (0, s, 0, h))
    pair = pl.BlockSpec((2, span, cols), lambda h, *_: (0, 0, h))
    stat = pl.BlockSpec((some, 1, span), lambda h, *_: (h, 0, 0))
    both = pl.BlockSpec((2, 2, span, cols), lambda h, *_: (0, 0, 0, h))
    shapes = ((4, span, 1), (1, span), (span, 1), (1, span))
    ins = [(queries, head)] + [(kv, pair) for kv in kvs]
    ins += [(mark, whole(shape)) for mark, shape in zip(marks, shapes)]
    return head, stat, both, ins, span, heads, some


def attend(order, queries, s, kvs, marks, sofar):
    head, stat, both, ins, span, heads, some = attend_ins(queries, s, kvs, marks)
    return order.call(
        fwd_kernel,
        "attend",
        (heads // some,),
        ins,
        [(queries.shape, BF16, head), ((heads, 1, span), F32, stat)],
        [
            pltpu.VMEM((some, 1, span), F32),
            pltpu.VMEM((some, 1, span), F32),
            pltpu.VMEM((some, HD, span), F32),
        ],
        flops=16 * heads * span * span * HD,
        alias=sofar,
    )


def attend_back(order, queries, s, kvs, marks, attended, grad_att, log_total, sofar):
    head, stat, both, ins, span, heads, some = attend_ins(queries, s, kvs, marks)
    pairs = (2, 2, span, heads * HD)
    return order.call(
        bwd_kernel,
        "attend_back",
        (heads // some,),
        ins + [(attended, head), (grad_att, head), (log_total, stat)],
        [(queries.shape, BF16, head), (pairs, BF16, both), (pairs, BF16, both)],
        [pltpu.VMEM((some, HD, span), F32), pltpu.VMEM((some, 1, span), F32)],
        flops=40 * heads * span * span * HD,
        alias=sofar,
    )


def add_pair(order, near, got):
    shape = near.shape[1:]

    def body(place, a, b, base, far):
        base[...] = a[0].astype(F32) + b[0].astype(F32)
        far[...] = (a[1].astype(F32) + b[1].astype(F32)).astype(BF16)

    return order.call(
        body,
        "add_pair",
        (1,),
        [(near, whole(near.shape)), (got, whole(near.shape))],
        [(shape, F32, whole(shape)), (shape, BF16, whole(shape))],
    )


def back_project(order, gq, bases, gots, weights, q_c, q_n, kv_c, kv_n, n, width):
    rows, local = gq.shape
    seqs = len(bases)
    block = rows // n
    part = block // seqs
    size = width // 4
    tile = min(size, 256)
    steps = size // tile

    def body(place, gq_ref, *refs):
        base_refs, got_refs = refs[:seqs], refs[seqs : 2 * seqs]
        a, c, qb, qd, kb, kd, gkv, *outs = refs[2 * seqs :]
        g = pl.program_id(0)

        @pl.when(g == 0)
        def _():
            for s in range(seqs):
                for k in range(n):
                    to, at = k * block + s * part, k * part
                    gkv[:, to : to + part, :] = (
                        base_refs[s][:, at : at + part, :]
                        + got_refs[s][:, at : at + part, :].astype(F32)
                    ).astype(BF16)

        grads = (gq_ref[...], gkv[0], gkv[1])
        mine = ((a, 0), (a, 1), (a, 2))
        mine_n = ((c, 0), (c, 1), (c, 2))
        far = ((qb, 0), (kb, 0), (kb, 1))
        far_n = ((qd, 0), (kd, 0), (kd, 1))
        for p, sources in enumerate((mine, far, mine_n, far_n)):
            total = None
            for grad, (ref, j) in zip(grads, sources):
                more = dot_t(grad, ref[j])
                total = more if total is None else total + more
            cols = pl.ds(pl.multiple_of(p * size + g * tile, tile), tile)
            put_rows(outs, block, n, cols, total.astype(BF16))

    near = [
        pl.BlockSpec(
            (3, tile, local), lambda g, place, h=h: (0, own_half(place, h) * steps + g, 0)
        )
        for h in (0, 1)
    ]
    one = pl.BlockSpec((1, tile, local), lambda g, place: (0, g, 0))
    two = pl.BlockSpec((2, tile, local), lambda g, place: (0, g, 0))
    shape = (2, rows, local)
    return order.call(
        body,
        "back_project",
        (steps,),
        [(gq, whole((rows, local)))]
        + [(a, whole(a.shape)) for a in (*bases, *gots)]
        + [(weights, near[0]), (weights, near[1])]
        + [(q_c, one), (q_n, one), (kv_c, two), (kv_n, two)],
        [(shape, BF16, whole(shape))] + row_outs(n, block, width),
        flops=6 * rows * local * width,
    )


def weight_grad_rows(order, lefts, rights, name, more=None):
    span, units = rights[0].shape
    count = 1 if more is None else 1 + more[0].shape[0]
    width = lefts[0][0][0].shape[1]
    part = span // len(lefts[0])
    size = width // 4
    total_lefts = sum(len(parts) for parts in lefts)
    pairs = len(lefts)
    given = list(rights) + list(more or [])

    def body(place, *refs):
        right_refs = refs[total_lefts : total_lefts + pairs]
        more_refs = refs[total_lefts + pairs : -3]
        keep, send, x = refs[-3:]
        gather_rows(refs[:total_lefts], x)
        q = pl.program_id(0)
        for j in range(count):
            total = None
            for s in range(pairs):
                right = more_refs[s][j - 1] if j else right_refs[s][...]
                product = t_dot(x[s * span : (s + 1) * span, :], right)
                total = product if total is None else total + product
            low = total.astype(BF16)

            @pl.when(q < 2)
            def _(j=j, low=low):
                keep[0, j] = low

            @pl.when(q >= 2)
            def _(j=j, low=low):
                send[0, j] = low

    shape = (2, count, size, units)
    block = (1, count, size, units)
    return order.call(
        body,
        name,
        (4,),
        [
            (a, pl.BlockSpec((part, size), lambda q, place, k=k: (k, q)))
            for parts in lefts
            for a, k in parts
        ]
        + [(a, whole(a.shape)) for a in given],
        [
            (shape, BF16, pl.BlockSpec(block, lambda q, place: (jnp.minimum(q, 1), 0, 0, 0))),
            (shape, BF16, pl.BlockSpec(block, lambda q, place: (jnp.maximum(q - 2, 0), 0, 0, 0))),
        ],
        [pltpu.VMEM((pairs * span, size), BF16)],
        flops=2 * count * pairs * span * units * width,
    )


def weight_grad_cols(order, lefts, rights, name):
    span, units = lefts[0].shape
    width = rights[0][0][0].shape[1]
    part = span // len(rights[0])
    size = width // 4
    tile = min(units, 256)
    pairs = len(lefts)

    def body(place, *refs):
        left_refs, right_refs = refs[:pairs], refs[pairs:-3]
        keep, send, y = refs[-3:]

        @pl.when(pl.program_id(0) == 0)
        def _():
            gather_rows(right_refs, y)

        total = None
        for s, ref in enumerate(left_refs):
            more = t_dot(ref[...], y[s * span : (s + 1) * span, :])
            total = more if total is None else total + more
        for q in range(4):
            (keep, send)[q // 2][q % 2, 0] = total[:, q * size : (q + 1) * size].astype(BF16)

    shape = (2, 1, units, size)
    out = pl.BlockSpec((2, 1, tile, size), lambda g, place: (0, 0, g, 0))
    return order.call(
        body,
        name,
        (units // tile,),
        [(a, pl.BlockSpec((span, tile), lambda g, place: (0, g))) for a in lefts]
        + [item for parts in rights for item in row_ins(parts, part, width)],
        [(shape, BF16, out), (shape, BF16, out)],
        [pltpu.VMEM((pairs * span, width), BF16)],
        flops=2 * pairs * span * units * width,
    )


class WeightSum:
    def __init__(self, order, keep, send):
        self.order = order
        self.keep = keep
        self.got = core_swap(send)
        self.shape = keep.shape[1:]

    def add(self, items, name):
        count, rows, cols = self.shape
        tile = min(rows, 512)

        def body(place, *refs):
            total = refs[0][...].astype(F32)
            for ref in refs[1:-1]:
                total = total + ref[...].astype(F32)
            refs[-1][...] = total.astype(BF16).reshape(refs[-1].shape)

        def quarter(k):
            return pl.BlockSpec((1, 1, tile, cols), lambda j, i, place: (k, j, i, 0))

        plain = pl.BlockSpec((1, tile, cols), lambda j, i, place: (j, i, 0))
        ins = []
        for array, k in items:
            if k is None:
                ins.append((array[None], pl.BlockSpec((1, 1, tile, cols), lambda j, i, place: (0, j, i, 0))))
            else:
                ins.append((array, quarter(k)))
        return self.order.call(
            body, name, (count, rows // tile), ins, [(self.shape, BF16, plain)]
        )[0]

    def to_x(self):
        self.got_x = x_swap(self.add([(self.keep, 1), (self.got, 1)], "sum_core"))

    def to_y(self):
        self.four = self.add([(self.keep, 0), (self.got, 0), (self.got_x, None)], "sum_x")
        self.got_y = y_swap(self.four)

    def to_core(self):
        self.total = self.add([(self.four, None), (self.got_y, None)], "sum_y")
        self.other = core_swap(self.total)

    def finish(self, axis, base=0, full=None, sofar=None):
        count, rows, cols = self.shape
        tile = min(rows, 512)
        steps = rows // tile

        def body(place, a, b, out):
            mine = jnp.full(a.shape, (pl.program_id(0) == place[0]).astype(jnp.int32)) > 0
            out[...] = jnp.where(mine, a[...].astype(F32), b[...].astype(F32))

        block = (1, tile, cols)
        source = pl.BlockSpec(block, lambda h, j, i, place: (j, i, 0))
        if axis == 0:
            shape = (full or count, 2 * rows, cols)
            spec = pl.BlockSpec(block, lambda h, j, i, place: (base + j, h * steps + i, 0))
        else:
            shape = (full or count, rows, 2 * cols)
            spec = pl.BlockSpec(block, lambda h, j, i, place: (base + j, i, h))
        return self.order.call(
            body,
            "finish",
            (2, count, steps),
            [(self.total, source), (self.other, source)],
            [(shape, F32, spec)],
            alias=sofar,
        )[0]


def out_rows(order, mid, summed, bias):
    seqs, part, width = summed.shape
    size = width // 4

    def body(place, mid_ref, sum_ref, bias_ref, out, line):
        for s in range(seqs):
            rows = slice(s * part, (s + 1) * part)
            line[...] = (mid_ref[rows] + sum_ref[s].astype(F32) + bias_ref[...]).astype(BF16)
            for p in range(4):
                cols = pl.ds(pl.multiple_of(natural_of(place, p) * size, size), size)
                out[s, :, cols] = line[:, p * size : (p + 1) * size]

    shape = (seqs, part, width)
    return order.call(
        body,
        "out_rows",
        (1,),
        [(mid, whole(mid.shape)), (summed, whole(shape)), (bias, whole((1, width)))],
        [(shape, BF16, whole(shape))],
        [pltpu.VMEM((part, width), BF16)],
    )[0]


def assemble(order, blocks, seqs, block):
    n = len(blocks)
    width = blocks[0][0].shape[1]
    part = block // seqs

    def body(place, *refs):
        out = refs[-1]
        for k in range(n):
            rows = pl.ds(pl.multiple_of((place[2] ^ k) * part, part), part)
            for s in range(seqs):
                out[s, rows, :] = refs[k][s * part : (s + 1) * part]

    shape = (seqs, n * part, width)
    return order.call(
        body,
        "assemble",
        (1,),
        row_ins(blocks, block, width),
        [(shape, BF16, whole(shape))],
    )[0]


def sum_first(parts):
    return tp_swap(parts[-1], 1)


def sum_second(order, parts, got, n, block):
    keep = parts[0]
    if n == 2:
        return [(keep, 0), (got, 0)]
    if n == 4:
        passed = add_rows(order, (keep, 1), (got, 0), block)
        return [(keep, 0), (tp_swap(passed, 2), 0), (tp_swap(parts[1], 1), 0)]
    total = (keep.astype(F32) + got.astype(F32)).astype(BF16)
    held = [total[k * block : (k + 1) * block] for k in range(n // 2)]
    bit = 2
    while bit < n:
        got = tp_swap(jnp.concatenate(held[1::2], axis=0), bit)
        held = [
            (a.astype(F32) + got[j * block : (j + 1) * block].astype(F32)).astype(BF16)
            for j, a in enumerate(held[::2])
        ]
        bit *= 2
    return [(held[0], 0)]


class Gather:
    def __init__(self, order, own):
        self.order = order
        self.own = own
        self.n = lax.axis_size("tp")
        if self.n == 4:
            self.far = tp_swap(own, 2)
            self.near = tp_swap(own, 1)

    def pass_on(self):
        if self.n == 4:
            self.far, self.near = self.order.tie(self.far, self.near)
            self.last = tp_swap(self.far, 1)

    def blocks(self):
        if self.n == 4:
            return [(a, 0) for a in (self.own, self.near, self.far, self.last)]
        blocks = [self.own]
        size = self.own.shape[0]
        bit = 1
        while bit < self.n:
            got = tp_swap(jnp.concatenate(blocks, axis=0), bit)
            blocks = blocks + [got[k * size : (k + 1) * size] for k in range(bit)]
            bit *= 2
        return [(block, 0) for block in blocks]


def sum_pairs(values):
    values = values + core_swap(values)
    values = values + y_swap(values)
    return values + x_swap(values)


def local(
    block_in,
    segments,
    out_grad,
    ln1_gain,
    ln1_bias,
    w_qkv,
    b_qv,
    w_attn_out,
    b_attn_out,
    ln2_gain,
    ln2_bias,
    w_up,
    b_up,
    w_down,
    b_down,
):
    seqs, span, width = block_in.shape
    n = lax.axis_size("tp")
    cx = lax.axis_index("ctx")
    blocks = lax.axis_size("ctx")
    z = lax.axis_index("tp")
    part = span // n
    local_width = w_qkv.shape[2]
    each = range(seqs)

    place = jnp.stack(
        [cx & 1, lax.axis_index("fsdp"), z, cx] + [(cx ^ b) <= cx for b in range(blocks)]
    ).astype(jnp.int32)
    order = Order(place)

    w3 = jnp.transpose(w_qkv, (1, 0, 2))
    wo, wu, wd = w_attn_out[None], w_up[None], w_down[None]

    def vector(values):
        return values.astype(F32)[None]

    gain_one = to_relative(vector(ln1_gain))
    gain_two = to_relative(vector(ln2_gain))
    shift_two = to_relative(vector(ln2_bias))
    bias_out = to_relative(vector(b_attn_out))
    bias_down = to_relative(vector(b_down))
    bias_kv = jnp.stack([jnp.zeros_like(b_qv[1:]), b_qv[1:]])
    bias_q = b_qv[None, :1]

    block = seqs * part
    kv_c = x_swap(take_half(order, w3, 1, 2, 0))
    n1, own_x = norm_in(order, block_in, vector(ln1_gain), vector(ln1_bias), n)
    n1_split = by_sequence(n1, n, seqs)
    kv_c = order.tie(kv_c)
    kv_n = core_swap(kv_c)
    q_c = x_swap(take_half(order, w3, 0, 1, 0))

    spot = mix_rows(jnp.arange(span, dtype=jnp.int32))
    marks, valid = [], []
    for s in each:
        valid.append((piece(segments[s], cx * span, span, 0) != 0).astype(F32)[:, None])
        key_seg = jnp.stack(
            [mix_rows(piece(segments[s], (cx ^ b) * span, span, 0)) for b in range(blocks)]
        )
        marks.append((key_seg[:, :, None], key_seg[0][None, :], spot[:, None], spot[None, :]))

    kvs = [
        project(order, (n1_split, s), w3, 1, kv_c, kv_n, bias_kv, "project_kv") for s in each
    ]
    kv_y = [y_swap(kvs[0])]
    o_c = x_swap(take_half(order, wo, 0, 1, 1))
    cot = cot_in(order, out_grad, jnp.stack(valid), n)
    q_c = order.tie(q_c)
    q_n = core_swap(q_c)
    d_c = x_swap(take_half(order, wd, 0, 1, 1))
    queries = by_sequence(
        project(order, n1, w3, 0, q_c, q_n, bias_q, "project_q")[0], n, seqs
    )
    o_c = order.tie(o_c)
    o_n = core_swap(o_c)
    kv_all, log_total = [], []
    attended = None
    for s in each:
        kv2 = order.tie(kv_y[s])
        kv_all.append((kvs[s], core_swap(kvs[s]), kv2, core_swap(kv2)))
        if s + 1 < seqs:
            kvs[s + 1] = order.tie(kvs[s + 1])
            kv_y.append(y_swap(kvs[s + 1]))
        attended, total = attend(order, queries, s, kv_all[s], marks[s], attended)
        log_total.append(total)
    flat_attended = attended.reshape(seqs * span, local_width)

    pieces, steps = col_pieces(wo, o_c, o_n, 256)
    parts = to_features(
        order, flat_attended, pieces, steps, 256, False, n, width, "attn_out"
    )
    got = sum_first(parts)
    d_c = order.tie(d_c)
    d_n = core_swap(d_c)
    u_c = x_swap(take_half(order, wu, 0, 1, 0))
    grad_active = active_grad(order, cot, wd, d_c, d_n)
    parts = sum_second(order, parts, got, n, block)
    middle, own = norm_mid(order, parts, own_x, bias_out, gain_two, shift_two)
    n2 = Gather(order, own)
    n2.pass_on()
    u_c = order.tie(u_c)
    u_n = core_swap(u_c)

    n2 = n2.blocks()
    up_sums, active, grad_hidden = feed(
        order, n2, wu, u_c, u_n, vector(b_up), grad_active
    )
    pieces, steps = row_pieces(wu, u_c, u_n, 256)
    parts = to_features(order, grad_hidden, pieces, steps, 256, True, n, width, "grad_n2")
    got = sum_first(parts)
    pieces, steps = col_pieces(wd, d_c, d_n, 256)
    (out_part,) = to_features(
        order, active, pieces, steps, 256, False, n, width, "feed_out", seqs
    )
    parts = sum_second(order, parts, got, n, block)
    w_down_sum = WeightSum(
        order, *weight_grad_cols(order, [active], [[(cot, 0)]], "grad_w_down")
    )
    stats_two, grad_mid, own = back_mid(order, parts, middle, cot, gain_two)
    gm = Gather(order, own)
    w_up_sum = WeightSum(order, *weight_grad_rows(order, [n2], [grad_hidden], "grad_w_up"))
    gm.pass_on()
    out_part = order.tie(out_part)
    out_sum = lax.psum_scatter(out_part, "tp", scatter_dimension=1, tiled=True)

    gm = gm.blocks()
    grad_att = by_sequence(heads_grad(order, gm, seqs * span, wo, o_c, o_n), n, seqs)
    near, got, bases, fars = [], [], [], []
    g_q = None

    def pair_back(s):
        base, far = add_pair(order, near[s], got[s])
        bases.append(base)
        fars.append(y_swap(far))

    for s in each:
        g_q, close, away = attend_back(
            order, queries, s, kv_all[s], marks[s], attended, grad_att, log_total[s], g_q
        )
        near.append(close)
        got.append(core_swap(away))
        if s == 0:
            w_down_sum.to_x()
        if s + 1 < seqs:
            pair_back(s)
    w_out_sum = WeightSum(order, *weight_grad_cols(order, [flat_attended], [gm], "grad_w_attn"))
    w_up_sum.to_x()
    pair_back(seqs - 1)
    g_q = g_q.reshape(seqs * span, local_width)
    g_kv, *parts = back_project(
        order, g_q, bases, fars, w3, q_c, q_n, kv_c, kv_n, n, width
    )
    got = sum_first(parts)
    w_qkv_sum = WeightSum(
        order, *weight_grad_rows(order, [[(n1, 0)]], [g_q], "grad_w_qkv", [g_kv])
    )
    w_down_sum.to_y()
    parts = sum_second(order, parts, got, n, block)
    w_up_sum.to_y()
    w_qkv_sum.to_x()
    w_down_sum.to_core()
    stats_one, own = back_in(order, parts, own_x, grad_mid, gain_one)
    in_rows = Gather(order, own)

    def over_rows(values):
        return jnp.sum(values.astype(F32), axis=0)

    tall = to_natural(jnp.concatenate([stats_two[:4], stats_one[:2]])).reshape(-1)
    narrow = jnp.concatenate([over_rows(g_q), over_rows(g_kv[1]), up_sums[0]])
    packed = jnp.concatenate([tall, narrow])
    w_qkv_sum.to_y()
    w_up_sum.to_core()
    in_rows.pass_on()
    out_own = out_rows(order, middle, out_sum, bias_down)
    block_out = lax.all_gather(out_own, "tp", axis=1, tiled=True)
    g_down = w_down_sum.finish(1)[0]
    w_out_sum.to_x()
    packed = packed + order.tie(core_swap(packed))
    g_up = w_up_sum.finish(0)[0]
    w_qkv_sum.to_core()
    w_out_sum.to_y()
    packed = packed + order.tie(x_swap(packed))
    g_qkv = jnp.transpose(w_qkv_sum.finish(0), (1, 0, 2))
    packed = packed + order.tie(y_swap(packed))
    w_out_sum.to_core()
    in_grad = assemble(order, in_rows.blocks(), seqs, block)
    g_out = w_out_sum.finish(1)[0]
    tall = packed[: 6 * width]
    bit = 1
    while bit < n:
        tall = tall + tp_swap(tall, bit)
        bit *= 2
    early = tall.reshape(6, width)
    late = early[4:]
    narrow = packed[6 * width :]
    g_bqv = narrow[: 2 * local_width].reshape(2, local_width)
    g_bup = narrow[2 * local_width :]
    return (
        block_out,
        in_grad,
        late[0],
        late[1],
        g_qkv,
        g_bqv,
        g_out,
        early[0],
        early[1],
        early[2],
        g_up,
        g_bup,
        g_down,
        early[3],
    )


def solution(mesh):
    in_specs = (
        P("fsdp", "ctx", None),
        P("fsdp", None),
        P("fsdp", "ctx", None),
        P(),
        P(),
        P("fsdp", None, "tp"),
        P(None, "tp"),
        P("tp", "fsdp"),
        P(),
        P(),
        P(),
        P("fsdp", "tp"),
        P("tp"),
        P("tp", "fsdp"),
        P(),
    )
    out_specs = (
        P("fsdp", "ctx", None),
        P("fsdp", "ctx", None),
        P(),
        P(),
        P("fsdp", None, "tp"),
        P(None, "tp"),
        P("tp", "fsdp"),
        P(),
        P(),
        P(),
        P("fsdp", "tp"),
        P("tp"),
        P("tp", "fsdp"),
        P(),
    )
    return jax.shard_map(local, mesh=mesh, in_specs=in_specs, out_specs=out_specs, check_vma=False)
```

```python
import jax
import jax.numpy as jnp
from jax import lax
from jax.experimental import pallas as pl
from jax.experimental.pallas import tpu as pltpu
from jax.sharding import PartitionSpec as P

HD = 128
NORM_EPS = 1e-05
MASKED = -1e30
LOG2E = 1.4426950408889634
F32 = jnp.float32
BF16 = jnp.bfloat16

ROOM = 40 * 2**20
X_SWAP = [(0, 1), (1, 0)]
ANY = pl.BlockSpec(memory_space=pl.ANY)


def xor_pairs(count, bit):
    return [(j, j ^ bit) for j in range(count)]


def core_swap(values):
    return lax.ppermute(values, "ctx", xor_pairs(lax.axis_size("ctx"), 1))


def y_swap(values):
    return lax.ppermute(values, "ctx", xor_pairs(lax.axis_size("ctx"), 2))


def x_swap(values):
    return lax.ppermute(values, "fsdp", X_SWAP)


def tp_swap(values, bit):
    return lax.ppermute(values, "tp", xor_pairs(lax.axis_size("tp"), bit))


def norm_parts(values):
    centred = values - jnp.mean(values, axis=-1, keepdims=True)
    norm_scale = lax.rsqrt(jnp.mean(centred * centred, axis=-1, keepdims=True) + NORM_EPS)
    return (centred * norm_scale, norm_scale)


def norm_back(grad_norm, gain, normed, norm_scale):
    lifted = grad_norm * gain
    return norm_scale * (
        lifted
        - jnp.mean(lifted, axis=-1, keepdims=True)
        - normed * jnp.mean(lifted * normed, axis=-1, keepdims=True)
    )


def dot(a, b):
    return jnp.dot(a, b, preferred_element_type=F32)


def dot_t(a, b):
    return lax.dot_general(a, b, (((1,), (1,)), ((), ())), preferred_element_type=F32)


def t_dot(a, b):
    return lax.dot_general(a, b, (((0,), (0,)), ((), ())), preferred_element_type=F32)


def piece(values, start, count, axis):
    return lax.dynamic_slice_in_dim(values, start, count, axis)


def to_relative(values):
    i, c = lax.axis_index("fsdp"), lax.axis_index("ctx") & 1
    size = values.shape[-1] // 4
    axis = values.ndim - 1
    return jnp.concatenate(
        [piece(values, (((k & 1) ^ i) * 2 + ((k >> 1) ^ c)) * size, size, axis) for k in range(4)],
        axis=axis,
    )


def to_natural(values):
    i, c = lax.axis_index("fsdp"), lax.axis_index("ctx") & 1
    size = values.shape[-1] // 4
    axis = values.ndim - 1
    return jnp.concatenate(
        [piece(values, (((b >> 1) ^ i) + 2 * ((b & 1) ^ c)) * size, size, axis) for b in range(4)],
        axis=axis,
    )


def mix_rows(values):
    n = lax.axis_size("tp")
    z = lax.axis_index("tp")
    size = values.shape[0] // n
    return jnp.concatenate([piece(values, (z ^ k) * size, size, 0) for k in range(n)], axis=0)


class Order:
    def __init__(self, place):
        self.place = place
        self.last = None

    def call(self, body, name, grid, ins, outs, scratch=(), flops=0, after=(), alias=None):
        spare = list(after)
        if self.last is not None and self.last is not alias:
            spare.append(self.last)
        if alias is not None:
            spare.append(alias)
        first = 1 + len(ins)

        def kernel(*refs):
            body(*refs[:first], *refs[first + len(spare) :])

        moved = sum(a.size * a.dtype.itemsize for a, unused in ins)
        moved += sum(2 * jnp.dtype(d).itemsize * len(s) for s, d, unused in outs)
        result = pl.pallas_call(
            kernel,
            grid_spec=pltpu.PrefetchScalarGridSpec(
                num_scalar_prefetch=1,
                grid=grid,
                in_specs=[spec for unused, spec in ins] + [ANY] * len(spare),
                out_specs=[spec for unused, also, spec in outs],
                scratch_shapes=list(scratch),
            ),
            out_shape=[jax.ShapeDtypeStruct(s, d) for s, d, unused in outs],
            input_output_aliases={} if alias is None else {len(ins) + len(spare): 0},
            compiler_params=pltpu.CompilerParams(vmem_limit_bytes=ROOM),
            cost_estimate=pl.CostEstimate(
                flops=int(flops), bytes_accessed=int(moved), transcendentals=0
            ),
            name=name,
        )(self.place, *[a for a, unused in ins], *spare)
        self.last = result[-1]
        return result

    def tie(self, *values):
        count = len(values)

        def kernel(place, *refs):
            del place, refs

        tied = pl.pallas_call(
            kernel,
            grid_spec=pltpu.PrefetchScalarGridSpec(
                num_scalar_prefetch=1,
                grid=(1,),
                in_specs=[ANY] * (count + 1),
                out_specs=[ANY] * count,
            ),
            out_shape=[jax.ShapeDtypeStruct(a.shape, a.dtype) for a in values],
            input_output_aliases={1 + k: k for k in range(count)},
            name="tie",
        )(self.place, *values, self.last)
        self.last = tied[0]
        return tied if count > 1 else tied[0]


def whole(shape):
    return pl.BlockSpec(shape, lambda *_: (0,) * len(shape))


def natural_of(place, k):
    return ((k & 1) ^ place[1]) * 2 + ((k >> 1) ^ place[0])


def own_half(place, which):
    return place[0] if which == 0 else 1 - place[0]


def take_half(order, weight, base, count, axis, after=()):
    unused, rows, cols = weight.shape
    if axis == 0:
        rows = rows // 2
    else:
        cols = cols // 2
    tile = min(rows, 512)

    def body(place, src, dst):
        dst[...] = src[...]

    def spot(g, i, place):
        if axis == 0:
            return (base + g, place[0] * (rows // tile) + i, 0)
        return (base + g, i, place[0])

    block = (1, tile, cols)
    return order.call(
        body,
        "take_half",
        (count, rows // tile),
        [(weight, pl.BlockSpec(block, spot))],
        [((count, rows, cols), BF16, pl.BlockSpec(block, lambda g, i, place: (g, i, 0)))],
        after=after,
    )[0]


def norm_in(order, block_in, gain, shift, n):
    seqs, span, width = block_in.shape
    part = span // n
    size = width // 4

    def body(place, src, gain_ref, shift_ref, normed_ref, own_ref, line):
        for k in range(n):
            rows = pl.ds(pl.multiple_of((place[2] ^ k) * part, part), part)
            for s in range(seqs):
                values = src[s, rows, :].astype(F32)
                normed, unused = norm_parts(values)
                line[...] = (normed * gain_ref[...] + shift_ref[...]).astype(BF16)
                to = (k * seqs + s) * part
                for p in range(4):
                    cols = pl.ds(pl.multiple_of(natural_of(place, p) * size, size), size)
                    normed_ref[to : to + part, p * size : (p + 1) * size] = line[:, cols]
                    if k == 0:
                        own_ref[to : to + part, p * size : (p + 1) * size] = src[s, rows, cols]

    return order.call(
        body,
        "norm_in",
        (1,),
        [
            (block_in, whole(block_in.shape)),
            (gain, whole((1, width))),
            (shift, whole((1, width))),
        ],
        [
            ((seqs * span, width), BF16, whole((seqs * span, width))),
            ((seqs * part, width), BF16, whole((seqs * part, width))),
        ],
        [pltpu.VMEM((part, width), BF16)],
    )


def cot_in(order, out_grad, valid, n):
    seqs, span, width = out_grad.shape
    part = span // n
    size = width // 4

    def body(place, src, valid_ref, cot_ref):
        for k in range(n):
            rows = pl.ds(pl.multiple_of((place[2] ^ k) * part, part), part)
            for s in range(seqs):
                to = (k * seqs + s) * part
                for p in range(4):
                    cols = pl.ds(pl.multiple_of(natural_of(place, p) * size, size), size)
                    values = src[s, rows, cols].astype(F32) * valid_ref[s, rows, :]
                    cot_ref[to : to + part, p * size : (p + 1) * size] = values.astype(BF16)

    shape = (seqs * span, width)
    return order.call(
        body,
        "cot_in",
        (1,),
        [(out_grad, whole(out_grad.shape)), (valid, whole(valid.shape))],
        [(shape, BF16, whole(shape))],
    )[0]


def by_sequence(values, n, seqs):
    rows, width = values.shape
    return values.reshape(n, seqs, rows // n // seqs, width)


def project(order, n1, weights, base, far_c, far_n, bias, name):
    count, size, local = far_c.shape
    one = isinstance(n1, tuple)
    if one:
        values, s = n1
        n, unused, part, width = values.shape
        rows = n * part
        spec = pl.BlockSpec((n, 1, part, width), lambda g, place: (0, s, 0, 0))
    else:
        values = n1
        rows, width = values.shape
        spec = whole((rows, width))

    def body(place, x, a, b, c, d, bias_ref, out):
        total = bias_ref[0].astype(F32)
        for p, ref in enumerate((a, b, c, d)):
            cols = slice(p * size, (p + 1) * size)
            some = x[:, 0, :, cols].reshape(rows, size) if one else x[:, cols]
            total = total + dot(some, ref[0])
        out[0] = total.astype(BF16)

    block = (1, size, local)
    near = [
        pl.BlockSpec(block, lambda g, place, h=h: (base + g, own_half(place, h), 0)) for h in (0, 1)
    ]
    away = pl.BlockSpec(block, lambda g, place: (g, 0, 0))
    return order.call(
        body,
        name,
        (count,),
        [
            (values, spec),
            (weights, near[0]),
            (far_c, away),
            (weights, near[1]),
            (far_n, away),
            (bias, pl.BlockSpec((1, 1, local), lambda g, place: (g, 0, 0))),
        ],
        [((count, rows, local), BF16, pl.BlockSpec((1, rows, local), lambda g, place: (g, 0, 0)))],
        flops=2 * rows * width * local * count,
    )[0]


def row_ins(parts, part, width):
    return [
        (array, pl.BlockSpec((part, width), lambda *_, k=k: (k, 0))) for array, k in parts
    ]


def row_outs(n, block, width):
    counts = (2, 1, 1) if n == 4 else (n // 2, n // 2)
    return [((c * block, width), BF16, whole((c * block, width))) for c in counts]


def put_rows(outs, block, n, cols, rows):
    for k in range(n):
        which, spot = (k % 2, k // 2)
        if n == 4 and which:
            which, spot = 1 + spot, 0
        outs[which][spot * block : (spot + 1) * block, cols] = rows[k * block : (k + 1) * block]


def col_pieces(weight, far_c, far_n, tile):
    unused, units, size = far_c.shape
    steps = size // tile
    block = (1, units, tile)
    near = [
        pl.BlockSpec(block, lambda g, place, h=h: (0, 0, own_half(place, h) * steps + g))
        for h in (0, 1)
    ]
    away = pl.BlockSpec(block, lambda g, place: (0, 0, g))
    return [(weight, near[0]), (far_c, away), (weight, near[1]), (far_n, away)], steps


def row_pieces(weight, far_c, far_n, tile):
    unused, size, units = far_c.shape
    steps = size // tile
    block = (1, tile, units)
    near = [
        pl.BlockSpec(block, lambda g, place, h=h: (0, own_half(place, h) * steps + g, 0))
        for h in (0, 1)
    ]
    away = pl.BlockSpec(block, lambda g, place: (0, g, 0))
    return [(weight, near[0]), (far_c, away), (weight, near[1]), (far_n, away)], steps


def to_features(order, values, pieces, steps, tile, turned, n, width, name, seqs=None):
    rows, units = values.shape
    block = rows // n
    size = width // 4
    times = dot_t if turned else dot

    def body(place, x, a, b, c, d, *outs):
        g = pl.program_id(0)
        for p, ref in enumerate((a, b, c, d)):
            got = times(x[...], ref[0]).astype(BF16)
            cols = pl.ds(pl.multiple_of(p * size + g * tile, tile), tile)
            if not seqs:
                put_rows(outs, block, n, cols, got)
                continue
            part = block // seqs
            for k in range(n):
                spot = pl.ds(pl.multiple_of((place[2] ^ k) * part, part), part)
                for s in range(seqs):
                    start = k * block + s * part
                    outs[0][s, spot, cols] = got[start : start + part]

    outs = row_outs(n, block, width)
    if seqs:
        shape = (seqs, rows // seqs, width)
        outs = [(shape, BF16, whole(shape))]
    return order.call(
        body,
        name,
        (steps,),
        [(values, whole((rows, units)))] + pieces,
        outs,
        flops=2 * rows * units * width,
    )


def add_rows(order, a, b, block):
    width = a[0].shape[1]

    def body(place, x, y, out):
        out[...] = (x[...].astype(F32) + y[...].astype(F32)).astype(BF16)

    return order.call(
        body,
        "add_rows",
        (1,),
        row_ins([a, b], block, width),
        [((block, width), BF16, whole((block, width)))],
    )[0]


def sum_all(refs):
    total = refs[0][...].astype(F32)
    for ref in refs[1:]:
        total = total + ref[...].astype(F32)
    return total


def norm_mid(order, parts, own, bias, gain, shift):
    part, width = own.shape
    count = len(parts)

    def body(place, *refs):
        own_ref, bias_ref, gain_ref, shift_ref, mid_ref, normed_ref = refs[count:]
        mid = own_ref[...].astype(F32) + sum_all(refs[:count]) + bias_ref[...]
        mid_ref[...] = mid
        normed, unused = norm_parts(mid)
        normed_ref[...] = (normed * gain_ref[...] + shift_ref[...]).astype(BF16)

    block, line = whole((part, width)), whole((1, width))
    return order.call(
        body,
        "norm_mid",
        (1,),
        row_ins(parts, part, width) + [(own, block), (bias, line), (gain, line), (shift, line)],
        [((part, width), F32, block), ((part, width), BF16, block)],
    )


def back_mid(order, parts, mid, cot, gain):
    part, width = mid.shape
    count = len(parts)

    def body(place, *refs):
        mid_ref, cot_ref, gain_ref, stats, grad_ref, low_ref = refs[count:]
        g2 = sum_all(refs[:count])
        normed, norm_scale = norm_parts(mid_ref[...])
        cotan = cot_ref[...].astype(F32)
        grad = cotan + norm_back(g2, gain_ref[...], normed, norm_scale)
        low = grad.astype(BF16)
        grad_ref[...] = grad
        low_ref[...] = low
        rows = (low.astype(F32), g2 * normed, g2, cotan)
        for k, values in enumerate(rows):
            stats[k : k + 1, :] = jnp.sum(values, axis=0, keepdims=True)
        stats[4:8, :] = jnp.zeros((4, width), F32)

    block, line = whole((part, width)), whole((1, width))
    return order.call(
        body,
        "back_mid",
        (1,),
        row_ins(parts, part, width) + [(mid, block), (cot, block), (gain, line)],
        [
            ((8, width), F32, whole((8, width))),
            ((part, width), F32, block),
            ((part, width), BF16, block),
        ],
    )


def back_in(order, parts, own, grad_mid, gain):
    part, width = own.shape
    count = len(parts)
    size = width // 4

    def body(place, *refs):
        own_ref, mid_ref, gain_ref, stats, low_ref, line = refs[count:]
        g1 = sum_all(refs[:count])
        normed, norm_scale = norm_parts(own_ref[...].astype(F32))
        grad = mid_ref[...] + norm_back(g1, gain_ref[...], normed, norm_scale)
        line[...] = grad.astype(BF16)
        for p in range(4):
            cols = pl.ds(pl.multiple_of(natural_of(place, p) * size, size), size)
            low_ref[:, cols] = line[:, p * size : (p + 1) * size]
        for k, values in enumerate((g1 * normed, g1)):
            stats[k : k + 1, :] = jnp.sum(values, axis=0, keepdims=True)
        stats[2:8, :] = jnp.zeros((6, width), F32)

    block, line = whole((part, width)), whole((1, width))
    return order.call(
        body,
        "back_in",
        (1,),
        row_ins(parts, part, width) + [(own, block), (grad_mid, block), (gain, line)],
        [((8, width), F32, whole((8, width))), ((part, width), BF16, block)],
        [pltpu.VMEM((part, width), BF16)],
    )


def gather_rows(refs, store):
    part = refs[0].shape[0]
    for k, ref in enumerate(refs):
        store[k * part : (k + 1) * part, :] = ref[...]


def active_grad(order, cot, weight, far_c, far_n):
    span, width = cot.shape
    units = weight.shape[1]
    size = width // 4
    tile = min(units, 512)

    def body(place, x, a, b, c, d, out):
        total = dot_t(x[:, :size], a[0])
        for p, ref in enumerate((b, c, d)):
            total = total + dot_t(x[:, (p + 1) * size : (p + 2) * size], ref[0])
        out[...] = total

    block = (1, tile, size)
    near = [pl.BlockSpec(block, lambda g, place, h=h: (0, g, own_half(place, h))) for h in (0, 1)]
    away = pl.BlockSpec(block, lambda g, place: (0, g, 0))
    return order.call(
        body,
        "active_grad",
        (units // tile,),
        [
            (cot, whole((span, width))),
            (weight, near[0]),
            (far_c, away),
            (weight, near[1]),
            (far_n, away),
        ],
        [((span, units), F32, pl.BlockSpec((span, tile), lambda g, place: (0, g)))],
        flops=2 * span * units * width,
    )[0]


def feed(order, n2_parts, weight, far_c, far_n, bias, grad_active):
    n = len(n2_parts)
    width = n2_parts[0][0].shape[1]
    span = cot_rows = grad_active.shape[0]
    part = cot_rows // n
    units = weight.shape[2]
    size = width // 4
    tile = min(units, 512)

    def body(place, *refs):
        a, b, c, d, bias_ref, ga_ref, sums, act_ref, gh_ref, x = refs[n:]

        @pl.when(pl.program_id(0) == 0)
        def _():
            gather_rows(refs[:n], x)

        rate = 0.7978845608028654
        step = min(tile, 256)
        for start in range(0, tile, step):
            cols = slice(start, start + step)
            hidden = bias_ref[:, cols] + dot(x[:, :size], a[0, :, cols])
            for p, ref in enumerate((b, c, d)):
                hidden = hidden + dot(x[:, (p + 1) * size : (p + 2) * size], ref[0, :, cols])
            square = hidden * hidden
            bend = jnp.tanh(hidden * (rate + rate * 0.044715 * square))
            half = 0.5 + 0.5 * bend
            act_ref[:, cols] = (hidden * half).astype(BF16)
            turn = half - half * bend
            slope = half + hidden * turn * (rate + rate * 0.134145 * square)
            gh = (ga_ref[:, cols] * slope).astype(BF16)
            gh_ref[:, cols] = gh
            sums[:, cols] = jnp.sum(gh.astype(F32), axis=0, keepdims=True)

    block = (1, size, tile)
    near = [pl.BlockSpec(block, lambda g, place, h=h: (0, own_half(place, h), g)) for h in (0, 1)]
    away = pl.BlockSpec(block, lambda g, place: (0, 0, g))
    cols = pl.BlockSpec((span, tile), lambda g, place: (0, g))
    line = pl.BlockSpec((1, tile), lambda g, place: (0, g))
    return order.call(
        body,
        "feed",
        (units // tile,),
        row_ins(n2_parts, part, width)
        + [
            (weight, near[0]),
            (far_c, away),
            (weight, near[1]),
            (far_n, away),
            (bias, line),
            (grad_active, cols),
        ],
        [((1, units), F32, line), ((span, units), BF16, cols), ((span, units), BF16, cols)],
        [pltpu.VMEM((span, width), BF16)],
        flops=2 * span * units * width,
    )


def heads_grad(order, gm_parts, span, weight, far_c, far_n):
    n = len(gm_parts)
    width = gm_parts[0][0].shape[1]
    part = span // n
    local = weight.shape[1]
    size = width // 4

    def body(place, *refs):
        a, b, c, d, out, x = refs[n:]
        gather_rows(refs[:n], x)
        total = dot_t(x[:, :size], a[0])
        for p, ref in enumerate((b, c, d)):
            total = total + dot_t(x[:, (p + 1) * size : (p + 2) * size], ref[0])
        out[...] = total.astype(BF16)

    pieces, unused = col_pieces(weight, far_c, far_n, size)
    return order.call(
        body,
        "heads_grad",
        (1,),
        row_ins(gm_parts, part, width) + pieces,
        [((span, local), BF16, whole((span, local)))],
        [pltpu.VMEM((span, width), BF16)],
        flops=2 * span * local * width,
    )[0]


def head_rows(ref, h):
    n, unused, part, size = ref.shape
    return ref[:, 0, :, h * HD : (h + 1) * HD].reshape(n * part, HD)


def put_head(ref, h, turned):
    n, unused, part, size = ref.shape
    ref[:, 0, :, h * HD : (h + 1) * HD] = turned.T.astype(BF16).reshape(n, part, HD)


def head_of(kv, j, h):
    return kv[j, :, h * HD : (h + 1) * HD]


def fwd_kernel(live, q, kv0, kv1, kv2, kv3, kseg, qseg, kpos, qpos, out, lse, m_s, l_s, acc_s):
    heads = range(q.shape[3] // HD)
    rate = HD ** (-0.5) * LOG2E

    def scores(kv, b, h):
        t = dot_t(head_of(kv, 0, h), head_rows(q, h)) * rate
        allowed = kseg[b] == qseg[...]
        if b == 0:
            allowed = allowed & (kpos[...] <= qpos[...])
        return jnp.where(allowed, t, MASKED)

    for h in heads:
        t = scores(kv0, 0, h)
        top = jnp.max(t, axis=0, keepdims=True)
        p = jnp.exp2(t - top)
        m_s[h] = top
        l_s[h] = jnp.sum(p, axis=0, keepdims=True)
        acc_s[h] = t_dot(head_of(kv0, 1, h), p.astype(BF16))
    for b, kv in ((1, kv1), (2, kv2), (3, kv3)):

        @pl.when(live[4 + b] > 0)
        def _(b=b, kv=kv):
            for h in heads:
                t = scores(kv, b, h)
                old = m_s[h]
                top = jnp.maximum(old, jnp.max(t, axis=0, keepdims=True))
                p = jnp.exp2(t - top)
                fade = jnp.exp2(old - top)
                m_s[h] = top
                l_s[h] = l_s[h] * fade + jnp.sum(p, axis=0, keepdims=True)
                acc_s[h] = acc_s[h] * fade + t_dot(head_of(kv, 1, h), p.astype(BF16))

    for h in heads:
        total = l_s[h]
        put_head(out, h, acc_s[h] / total)
        lse[h] = m_s[h] + jnp.log2(total)


def bwd_kernel(
    live,
    q,
    kv0,
    kv1,
    kv2,
    kv3,
    kseg,
    qseg,
    kpos,
    qpos,
    att,
    grad,
    lse,
    gq,
    near,
    far,
    gq_s,
    delta_s,
):
    heads = range(q.shape[3] // HD)
    rate = HD ** (-0.5) * LOG2E
    factor = HD ** (-0.5)

    def grads(kv, b, h):
        queries, grad_out, keys = head_rows(q, h), head_rows(grad, h), head_of(kv, 0, h)
        t = dot_t(keys, queries) * rate
        allowed = kseg[b] == qseg[...]
        if b == 0:
            allowed = allowed & (kpos[...] <= qpos[...])
        p = jnp.exp2(jnp.where(allowed, t, MASKED) - lse[h])
        gv = dot(p.astype(BF16), grad_out)
        gp = dot_t(head_of(kv, 1, h), grad_out)
        gs = (p * (gp - delta_s[h])).astype(BF16)
        gk = dot(gs, queries) * factor
        return gk.astype(BF16), gv.astype(BF16), t_dot(keys, gs)

    def put(place, slot, h, gk, gv):
        cols = slice(h * HD, (h + 1) * HD)
        place[slot, 0, :, cols] = gk
        place[slot, 1, :, cols] = gv

    for h in heads:
        product = head_rows(grad, h).astype(F32) * head_rows(att, h).astype(F32)
        delta_s[h] = jnp.sum(product.T, axis=0, keepdims=True)
    for h in heads:
        gk, gv, turned = grads(kv0, 0, h)
        put(near, 0, h, gk, gv)
        gq_s[h] = turned
    for b, kv, place, slot in ((1, kv1, far, 0), (2, kv2, near, 1), (3, kv3, far, 1)):

        @pl.when(live[4 + b] > 0)
        def _(b=b, kv=kv, place=place, slot=slot):
            for h in heads:
                gk, gv, turned = grads(kv, b, h)
                put(place, slot, h, gk, gv)
                gq_s[h] += turned

        @pl.when(live[4 + b] == 0)
        def _(place=place, slot=slot):
            place[slot] = jnp.zeros(place.shape[1:], BF16)

    for h in heads:
        put_head(gq, h, gq_s[h] * factor)


def attend_ins(queries, s, kvs, marks):
    n, unused, part, local = queries.shape
    span = n * part
    heads = local // HD
    some = min(heads, 2)
    cols = some * HD
    head = pl.BlockSpec((n, 1, part, cols), lambda h, *_: (0, s, 0, h))
    pair = pl.BlockSpec((2, span, cols), lambda h, *_: (0, 0, h))
    stat = pl.BlockSpec((some, 1, span), lambda h, *_: (h, 0, 0))
    both = pl.BlockSpec((2, 2, span, cols), lambda h, *_: (0, 0, 0, h))
    shapes = ((4, span, 1), (1, span), (span, 1), (1, span))
    ins = [(queries, head)] + [(kv, pair) for kv in kvs]
    ins += [(mark, whole(shape)) for mark, shape in zip(marks, shapes)]
    return head, stat, both, ins, span, heads, some


def attend(order, queries, s, kvs, marks, sofar):
    head, stat, both, ins, span, heads, some = attend_ins(queries, s, kvs, marks)
    return order.call(
        fwd_kernel,
        "attend",
        (heads // some,),
        ins,
        [(queries.shape, BF16, head), ((heads, 1, span), F32, stat)],
        [
            pltpu.VMEM((some, 1, span), F32),
            pltpu.VMEM((some, 1, span), F32),
            pltpu.VMEM((some, HD, span), F32),
        ],
        flops=16 * heads * span * span * HD,
        alias=sofar,
    )


def attend_back(order, queries, s, kvs, marks, attended, grad_att, log_total, sofar):
    head, stat, both, ins, span, heads, some = attend_ins(queries, s, kvs, marks)
    pairs = (2, 2, span, heads * HD)
    return order.call(
        bwd_kernel,
        "attend_back",
        (heads // some,),
        ins + [(attended, head), (grad_att, head), (log_total, stat)],
        [(queries.shape, BF16, head), (pairs, BF16, both), (pairs, BF16, both)],
        [pltpu.VMEM((some, HD, span), F32), pltpu.VMEM((some, 1, span), F32)],
        flops=40 * heads * span * span * HD,
        alias=sofar,
    )


def add_pair(order, near, got):
    shape = near.shape[1:]

    def body(place, a, b, base, far):
        base[...] = a[0].astype(F32) + b[0].astype(F32)
        far[...] = (a[1].astype(F32) + b[1].astype(F32)).astype(BF16)

    return order.call(
        body,
        "add_pair",
        (1,),
        [(near, whole(near.shape)), (got, whole(near.shape))],
        [(shape, F32, whole(shape)), (shape, BF16, whole(shape))],
    )


def back_project(order, gq, bases, gots, weights, q_c, q_n, kv_c, kv_n, n, width):
    rows, local = gq.shape
    seqs = len(bases)
    block = rows // n
    part = block // seqs
    size = width // 4
    tile = min(size, 256)
    steps = size // tile

    def body(place, gq_ref, *refs):
        base_refs, got_refs = refs[:seqs], refs[seqs : 2 * seqs]
        a, c, qb, qd, kb, kd, gkv, *outs = refs[2 * seqs :]
        g = pl.program_id(0)

        @pl.when(g == 0)
        def _():
            for s in range(seqs):
                for k in range(n):
                    to, at = k * block + s * part, k * part
                    gkv[:, to : to + part, :] = (
                        base_refs[s][:, at : at + part, :]
                        + got_refs[s][:, at : at + part, :].astype(F32)
                    ).astype(BF16)

        grads = (gq_ref[...], gkv[0], gkv[1])
        mine = ((a, 0), (a, 1), (a, 2))
        mine_n = ((c, 0), (c, 1), (c, 2))
        far = ((qb, 0), (kb, 0), (kb, 1))
        far_n = ((qd, 0), (kd, 0), (kd, 1))
        for p, sources in enumerate((mine, far, mine_n, far_n)):
            total = None
            for grad, (ref, j) in zip(grads, sources):
                more = dot_t(grad, ref[j])
                total = more if total is None else total + more
            cols = pl.ds(pl.multiple_of(p * size + g * tile, tile), tile)
            put_rows(outs, block, n, cols, total.astype(BF16))

    near = [
        pl.BlockSpec(
            (3, tile, local), lambda g, place, h=h: (0, own_half(place, h) * steps + g, 0)
        )
        for h in (0, 1)
    ]
    one = pl.BlockSpec((1, tile, local), lambda g, place: (0, g, 0))
    two = pl.BlockSpec((2, tile, local), lambda g, place: (0, g, 0))
    shape = (2, rows, local)
    return order.call(
        body,
        "back_project",
        (steps,),
        [(gq, whole((rows, local)))]
        + [(a, whole(a.shape)) for a in (*bases, *gots)]
        + [(weights, near[0]), (weights, near[1])]
        + [(q_c, one), (q_n, one), (kv_c, two), (kv_n, two)],
        [(shape, BF16, whole(shape))] + row_outs(n, block, width),
        flops=6 * rows * local * width,
    )


def weight_grad_rows(order, lefts, rights, name, more=None):
    span, units = rights[0].shape
    count = 1 if more is None else 1 + more[0].shape[0]
    width = lefts[0][0][0].shape[1]
    part = span // len(lefts[0])
    size = width // 4
    total_lefts = sum(len(parts) for parts in lefts)
    pairs = len(lefts)
    given = list(rights) + list(more or [])

    def body(place, *refs):
        right_refs = refs[total_lefts : total_lefts + pairs]
        more_refs = refs[total_lefts + pairs : -3]
        keep, send, x = refs[-3:]
        gather_rows(refs[:total_lefts], x)
        q = pl.program_id(0)
        for j in range(count):
            total = None
            for s in range(pairs):
                right = more_refs[s][j - 1] if j else right_refs[s][...]
                product = t_dot(x[s * span : (s + 1) * span, :], right)
                total = product if total is None else total + product
            low = total.astype(BF16)

            @pl.when(q < 2)
            def _(j=j, low=low):
                keep[0, j] = low

            @pl.when(q >= 2)
            def _(j=j, low=low):
                send[0, j] = low

    shape = (2, count, size, units)
    block = (1, count, size, units)
    return order.call(
        body,
        name,
        (4,),
        [
            (a, pl.BlockSpec((part, size), lambda q, place, k=k: (k, q)))
            for parts in lefts
            for a, k in parts
        ]
        + [(a, whole(a.shape)) for a in given],
        [
            (shape, BF16, pl.BlockSpec(block, lambda q, place: (jnp.minimum(q, 1), 0, 0, 0))),
            (shape, BF16, pl.BlockSpec(block, lambda q, place: (jnp.maximum(q - 2, 0), 0, 0, 0))),
        ],
        [pltpu.VMEM((pairs * span, size), BF16)],
        flops=2 * count * pairs * span * units * width,
    )


def weight_grad_cols(order, lefts, rights, name):
    span, units = lefts[0].shape
    width = rights[0][0][0].shape[1]
    part = span // len(rights[0])
    size = width // 4
    tile = min(units, 256)
    pairs = len(lefts)

    def body(place, *refs):
        left_refs, right_refs = refs[:pairs], refs[pairs:-3]
        keep, send, y = refs[-3:]

        @pl.when(pl.program_id(0) == 0)
        def _():
            gather_rows(right_refs, y)

        total = None
        for s, ref in enumerate(left_refs):
            more = t_dot(ref[...], y[s * span : (s + 1) * span, :])
            total = more if total is None else total + more
        for q in range(4):
            (keep, send)[q // 2][q % 2, 0] = total[:, q * size : (q + 1) * size].astype(BF16)

    shape = (2, 1, units, size)
    out = pl.BlockSpec((2, 1, tile, size), lambda g, place: (0, 0, g, 0))
    return order.call(
        body,
        name,
        (units // tile,),
        [(a, pl.BlockSpec((span, tile), lambda g, place: (0, g))) for a in lefts]
        + [item for parts in rights for item in row_ins(parts, part, width)],
        [(shape, BF16, out), (shape, BF16, out)],
        [pltpu.VMEM((pairs * span, width), BF16)],
        flops=2 * pairs * span * units * width,
    )


class WeightSum:
    def __init__(self, order, keep, send):
        self.order = order
        self.keep = keep
        self.got = core_swap(send)
        self.shape = keep.shape[1:]

    def add(self, items, name):
        count, rows, cols = self.shape
        tile = min(rows, 512)

        def body(place, *refs):
            total = refs[0][...].astype(F32)
            for ref in refs[1:-1]:
                total = total + ref[...].astype(F32)
            refs[-1][...] = total.astype(BF16).reshape(refs[-1].shape)

        def quarter(k):
            return pl.BlockSpec((1, 1, tile, cols), lambda j, i, place: (k, j, i, 0))

        plain = pl.BlockSpec((1, tile, cols), lambda j, i, place: (j, i, 0))
        ins = []
        for array, k in items:
            if k is None:
                ins.append((array[None], pl.BlockSpec((1, 1, tile, cols), lambda j, i, place: (0, j, i, 0))))
            else:
                ins.append((array, quarter(k)))
        return self.order.call(
            body, name, (count, rows // tile), ins, [(self.shape, BF16, plain)]
        )[0]

    def to_x(self):
        self.got_x = x_swap(self.add([(self.keep, 1), (self.got, 1)], "sum_core"))

    def to_y(self):
        self.four = self.add([(self.keep, 0), (self.got, 0), (self.got_x, None)], "sum_x")
        self.got_y = y_swap(self.four)

    def to_core(self):
        self.total = self.add([(self.four, None), (self.got_y, None)], "sum_y")
        self.other = core_swap(self.total)

    def finish(self, axis, base=0, full=None, sofar=None):
        count, rows, cols = self.shape
        tile = min(rows, 512)
        steps = rows // tile

        def body(place, a, b, out):
            mine = jnp.full(a.shape, (pl.program_id(0) == place[0]).astype(jnp.int32)) > 0
            out[...] = jnp.where(mine, a[...].astype(F32), b[...].astype(F32))

        block = (1, tile, cols)
        source = pl.BlockSpec(block, lambda h, j, i, place: (j, i, 0))
        if axis == 0:
            shape = (full or count, 2 * rows, cols)
            spec = pl.BlockSpec(block, lambda h, j, i, place: (base + j, h * steps + i, 0))
        else:
            shape = (full or count, rows, 2 * cols)
            spec = pl.BlockSpec(block, lambda h, j, i, place: (base + j, i, h))
        return self.order.call(
            body,
            "finish",
            (2, count, steps),
            [(self.total, source), (self.other, source)],
            [(shape, F32, spec)],
            alias=sofar,
        )[0]


def out_rows(order, mid, summed, bias):
    seqs, part, width = summed.shape
    size = width // 4

    def body(place, mid_ref, sum_ref, bias_ref, out, line):
        for s in range(seqs):
            rows = slice(s * part, (s + 1) * part)
            line[...] = (mid_ref[rows] + sum_ref[s].astype(F32) + bias_ref[...]).astype(BF16)
            for p in range(4):
                cols = pl.ds(pl.multiple_of(natural_of(place, p) * size, size), size)
                out[s, :, cols] = line[:, p * size : (p + 1) * size]

    shape = (seqs, part, width)
    return order.call(
        body,
        "out_rows",
        (1,),
        [(mid, whole(mid.shape)), (summed, whole(shape)), (bias, whole((1, width)))],
        [(shape, BF16, whole(shape))],
        [pltpu.VMEM((part, width), BF16)],
    )[0]


def assemble(order, blocks, seqs, block):
    n = len(blocks)
    width = blocks[0][0].shape[1]
    part = block // seqs

    def body(place, *refs):
        out = refs[-1]
        for k in range(n):
            rows = pl.ds(pl.multiple_of((place[2] ^ k) * part, part), part)
            for s in range(seqs):
                out[s, rows, :] = refs[k][s * part : (s + 1) * part]

    shape = (seqs, n * part, width)
    return order.call(
        body,
        "assemble",
        (1,),
        row_ins(blocks, block, width),
        [(shape, BF16, whole(shape))],
    )[0]


def sum_first(parts):
    return tp_swap(parts[-1], 1)


def sum_second(order, parts, got, n, block):
    keep = parts[0]
    if n == 2:
        return [(keep, 0), (got, 0)]
    if n == 4:
        passed = add_rows(order, (keep, 1), (got, 0), block)
        return [(keep, 0), (tp_swap(passed, 2), 0), (tp_swap(parts[1], 1), 0)]
    total = (keep.astype(F32) + got.astype(F32)).astype(BF16)
    held = [total[k * block : (k + 1) * block] for k in range(n // 2)]
    bit = 2
    while bit < n:
        got = tp_swap(jnp.concatenate(held[1::2], axis=0), bit)
        held = [
            (a.astype(F32) + got[j * block : (j + 1) * block].astype(F32)).astype(BF16)
            for j, a in enumerate(held[::2])
        ]
        bit *= 2
    return [(held[0], 0)]


class Gather:
    def __init__(self, order, own):
        self.order = order
        self.own = own
        self.n = lax.axis_size("tp")
        if self.n == 4:
            self.far = tp_swap(own, 2)
            self.near = tp_swap(own, 1)

    def pass_on(self):
        if self.n == 4:
            self.far, self.near = self.order.tie(self.far, self.near)
            self.last = tp_swap(self.far, 1)

    def blocks(self):
        if self.n == 4:
            return [(a, 0) for a in (self.own, self.near, self.far, self.last)]
        blocks = [self.own]
        size = self.own.shape[0]
        bit = 1
        while bit < self.n:
            got = tp_swap(jnp.concatenate(blocks, axis=0), bit)
            blocks = blocks + [got[k * size : (k + 1) * size] for k in range(bit)]
            bit *= 2
        return [(block, 0) for block in blocks]


def sum_pairs(values):
    values = values + core_swap(values)
    values = values + y_swap(values)
    return values + x_swap(values)


def local(
    block_in,
    segments,
    out_grad,
    ln1_gain,
    ln1_bias,
    w_qkv,
    b_qv,
    w_attn_out,
    b_attn_out,
    ln2_gain,
    ln2_bias,
    w_up,
    b_up,
    w_down,
    b_down,
):
    seqs, span, width = block_in.shape
    n = lax.axis_size("tp")
    cx = lax.axis_index("ctx")
    blocks = lax.axis_size("ctx")
    z = lax.axis_index("tp")
    part = span // n
    local_width = w_qkv.shape[2]
    each = range(seqs)

    place = jnp.stack(
        [cx & 1, lax.axis_index("fsdp"), z, cx] + [(cx ^ b) <= cx for b in range(blocks)]
    ).astype(jnp.int32)
    order = Order(place)

    w3 = jnp.transpose(w_qkv, (1, 0, 2))
    wo, wu, wd = w_attn_out[None], w_up[None], w_down[None]

    def vector(values):
        return values.astype(F32)[None]

    gain_one = to_relative(vector(ln1_gain))
    gain_two = to_relative(vector(ln2_gain))
    shift_two = to_relative(vector(ln2_bias))
    bias_out = to_relative(vector(b_attn_out))
    bias_down = to_relative(vector(b_down))
    bias_kv = jnp.stack([jnp.zeros_like(b_qv[1:]), b_qv[1:]])
    bias_q = b_qv[None, :1]

    block = seqs * part
    kv_c = x_swap(take_half(order, w3, 1, 2, 0))
    n1, own_x = norm_in(order, block_in, vector(ln1_gain), vector(ln1_bias), n)
    n1_split = by_sequence(n1, n, seqs)
    kv_c = order.tie(kv_c)
    kv_n = core_swap(kv_c)
    q_c = x_swap(take_half(order, w3, 0, 1, 0))

    spot = mix_rows(jnp.arange(span, dtype=jnp.int32))
    marks, valid = [], []
    for s in each:
        valid.append((piece(segments[s], cx * span, span, 0) != 0).astype(F32)[:, None])
        key_seg = jnp.stack(
            [mix_rows(piece(segments[s], (cx ^ b) * span, span, 0)) for b in range(blocks)]
        )
        marks.append((key_seg[:, :, None], key_seg[0][None, :], spot[:, None], spot[None, :]))

    kvs = [
        project(order, (n1_split, s), w3, 1, kv_c, kv_n, bias_kv, "project_kv") for s in each
    ]
    kv_y = [y_swap(kvs[0])]
    o_c = x_swap(take_half(order, wo, 0, 1, 1))
    cot = cot_in(order, out_grad, jnp.stack(valid), n)
    q_c = order.tie(q_c)
    q_n = core_swap(q_c)
    d_c = x_swap(take_half(order, wd, 0, 1, 1))
    queries = by_sequence(
        project(order, n1, w3, 0, q_c, q_n, bias_q, "project_q")[0], n, seqs
    )
    o_c = order.tie(o_c)
    o_n = core_swap(o_c)
    kv_all, log_total = [], []
    attended = None
    for s in each:
        kv2 = order.tie(kv_y[s])
        kv_all.append((kvs[s], core_swap(kvs[s]), kv2, core_swap(kv2)))
        if s + 1 < seqs:
            kvs[s + 1] = order.tie(kvs[s + 1])
            kv_y.append(y_swap(kvs[s + 1]))
        attended, total = attend(order, queries, s, kv_all[s], marks[s], attended)
        log_total.append(total)
    flat_attended = attended.reshape(seqs * span, local_width)

    pieces, steps = col_pieces(wo, o_c, o_n, 256)
    parts = to_features(
        order, flat_attended, pieces, steps, 256, False, n, width, "attn_out"
    )
    got = sum_first(parts)
    d_c = order.tie(d_c)
    d_n = core_swap(d_c)
    u_c = x_swap(take_half(order, wu, 0, 1, 0))
    grad_active = active_grad(order, cot, wd, d_c, d_n)
    parts = sum_second(order, parts, got, n, block)
    middle, own = norm_mid(order, parts, own_x, bias_out, gain_two, shift_two)
    n2 = Gather(order, own)
    n2.pass_on()
    u_c = order.tie(u_c)
    u_n = core_swap(u_c)

    n2 = n2.blocks()
    up_sums, active, grad_hidden = feed(
        order, n2, wu, u_c, u_n, vector(b_up), grad_active
    )
    pieces, steps = row_pieces(wu, u_c, u_n, 256)
    parts = to_features(order, grad_hidden, pieces, steps, 256, True, n, width, "grad_n2")
    got = sum_first(parts)
    pieces, steps = col_pieces(wd, d_c, d_n, 256)
    (out_part,) = to_features(
        order, active, pieces, steps, 256, False, n, width, "feed_out", seqs
    )
    parts = sum_second(order, parts, got, n, block)
    w_down_sum = WeightSum(
        order, *weight_grad_cols(order, [active], [[(cot, 0)]], "grad_w_down")
    )
    stats_two, grad_mid, own = back_mid(order, parts, middle, cot, gain_two)
    gm = Gather(order, own)
    w_up_sum = WeightSum(order, *weight_grad_rows(order, [n2], [grad_hidden], "grad_w_up"))
    gm.pass_on()
    out_part = order.tie(out_part)
    out_sum = lax.psum_scatter(out_part, "tp", scatter_dimension=1, tiled=True)

    gm = gm.blocks()
    grad_att = by_sequence(heads_grad(order, gm, seqs * span, wo, o_c, o_n), n, seqs)
    near, got, bases, fars = [], [], [], []
    g_q = None

    def pair_back(s):
        base, far = add_pair(order, near[s], got[s])
        bases.append(base)
        fars.append(y_swap(far))

    for s in each:
        g_q, close, away = attend_back(
            order, queries, s, kv_all[s], marks[s], attended, grad_att, log_total[s], g_q
        )
        near.append(close)
        got.append(core_swap(away))
        if s == 0:
            w_down_sum.to_x()
        if s + 1 < seqs:
            pair_back(s)
    w_out_sum = WeightSum(order, *weight_grad_cols(order, [flat_attended], [gm], "grad_w_attn"))
    w_up_sum.to_x()
    pair_back(seqs - 1)
    g_q = g_q.reshape(seqs * span, local_width)
    g_kv, *parts = back_project(
        order, g_q, bases, fars, w3, q_c, q_n, kv_c, kv_n, n, width
    )
    got = sum_first(parts)
    w_qkv_sum = WeightSum(
        order, *weight_grad_rows(order, [[(n1, 0)]], [g_q], "grad_w_qkv", [g_kv])
    )
    w_down_sum.to_y()
    parts = sum_second(order, parts, got, n, block)
    w_up_sum.to_y()
    w_qkv_sum.to_x()
    w_down_sum.to_core()
    stats_one, own = back_in(order, parts, own_x, grad_mid, gain_one)
    in_rows = Gather(order, own)

    def over_rows(values):
        return jnp.sum(values.astype(F32), axis=0)

    tall = to_natural(jnp.concatenate([stats_two[:4], stats_one[:2]])).reshape(-1)
    narrow = jnp.concatenate([over_rows(g_q), over_rows(g_kv[1]), up_sums[0]])
    packed = jnp.concatenate([tall, narrow])
    w_qkv_sum.to_y()
    w_up_sum.to_core()
    in_rows.pass_on()
    out_own = out_rows(order, middle, out_sum, bias_down)
    block_out = lax.all_gather(out_own, "tp", axis=1, tiled=True)
    g_down = w_down_sum.finish(1)[0]
    w_out_sum.to_x()
    packed = packed + order.tie(core_swap(packed))
    g_up = w_up_sum.finish(0)[0]
    w_qkv_sum.to_core()
    w_out_sum.to_y()
    packed = packed + order.tie(x_swap(packed))
    g_qkv = jnp.transpose(w_qkv_sum.finish(0), (1, 0, 2))
    packed = packed + order.tie(y_swap(packed))
    w_out_sum.to_core()
    in_grad = assemble(order, in_rows.blocks(), seqs, block)
    g_out = w_out_sum.finish(1)[0]
    tall = packed[: 6 * width]
    bit = 1
    while bit < n:
        tall = tall + tp_swap(tall, bit)
        bit *= 2
    early = tall.reshape(6, width)
    late = early[4:]
    narrow = packed[6 * width :]
    g_bqv = narrow[: 2 * local_width].reshape(2, local_width)
    g_bup = narrow[2 * local_width :]
    return (
        block_out,
        in_grad,
        late[0],
        late[1],
        g_qkv,
        g_bqv,
        g_out,
        early[0],
        early[1],
        early[2],
        g_up,
        g_bup,
        g_down,
        early[3],
    )


def solution(mesh):
    in_specs = (
        P("fsdp", "ctx", None),
        P("fsdp", None),
        P("fsdp", "ctx", None),
        P(),
        P(),
        P("fsdp", None, "tp"),
        P(None, "tp"),
        P("tp", "fsdp"),
        P(),
        P(),
        P(),
        P("fsdp", "tp"),
        P("tp"),
        P("tp", "fsdp"),
        P(),
    )
    out_specs = (
        P("fsdp", "ctx", None),
        P("fsdp", "ctx", None),
        P(),
        P(),
        P("fsdp", None, "tp"),
        P(None, "tp"),
        P("tp", "fsdp"),
        P(),
        P(),
        P(),
        P("fsdp", "tp"),
        P("tp"),
        P("tp", "fsdp"),
        P(),
    )
    return jax.shard_map(local, mesh=mesh, in_specs=in_specs, out_specs=out_specs, check_vma=False)
```
